32 devices in a mesh: seq: 16 (over z, x, core), head: 2 (over y).
Axes of the slice: x: 2, y: 2, z: 4, core: 2. Of those that a mesh axis runs over, the one named last changes fastest.
Arguments:
- query_states: bfloat16 [2048, 2048], P('seq', 'head'), may hold values from -24.5 to 24.5
- key_states: bfloat16 [2048, 512], P('seq', 'head'), may hold values from -10.5 to 10.5
- value_states: bfloat16 [2048, 512], P('seq', 'head'), may hold values from -6 to 6
- out_weight: bfloat16 [2048, 4096], P('head'), may hold values from -0.125 to 0.125
- block_docs: int32 [16], replicated, may hold values from 0 to 7, never falling along the last dimension, each value on 1 to 4 neighbouring positions
Outputs:
- mixed: bfloat16 [2048, 4096], P('seq', 'head')
The draws below stay inside these ranges and needn't reach their ends.
Inputs may be any that keep to these rules, and one draw needn't show every extreme that they name: `block_docs`: A document spans at most 4 blocks.
All inputs are finite; a program needn't handle non-finite values.
Results may differ from the reference program's by a relative error of at most 0.0095.
Values may be sent and summed in bfloat16 or wider, within the bound.
No kernel may reach another device: no remote copies, remote signals or barrier semaphores. Data moves between devices by JAX's collectives and lax.ppermute only.
A program may use at most 64 MiB of HBM per device.

```python
import math
import jax
import jax.numpy as jnp
import numpy as np
from jax import lax

D = 4096
HD = 128
QH = 16
KH = 4
BLK = 128
TOK_DEV = 128
TOKENS = 2048
NBLK = 16
MOST = 4
DOCS = 8
N_SEQ = 16
N_HEAD = 2


def base_keys(key):
    return jnp.clip(jax.random.normal(jax.random.fold_in(key, 11), (TOKENS, KH * HD), jnp.float32), -3.5, 3.5)


def draw_key_states(key, part):
    base = base_keys(key)
    return base.astype(jnp.bfloat16)


def draw_query_states(key, part):
    drawn = jnp.clip(jax.random.normal(jax.random.fold_in(key, 12), (TOKENS, QH * HD), jnp.float32), -3.5, 3.5)
    return drawn.astype(jnp.bfloat16)


def block_scale(rng, shape, shards, low, largest):
    level = 1.0
    for axis_at, parts in shards:
        steps = jax.random.uniform(jax.random.fold_in(jax.random.fold_in(rng, 6), axis_at), (parts,), jnp.float32, low / len(shards), largest / len(shards))
        level = level * jnp.repeat(jnp.exp(steps), shape[axis_at] // parts).reshape((-1,) + (1,) * (len(shape) - 1 - axis_at))
    return level


def length_profile(count, total, limit, skew):
    portions = [(1 << 20) // math.isqrt(rank ** skew) + 1 for rank in range(2, count + 1)]
    surplus, holding = total - limit - (count - 1), [1] * (count - 1)
    while surplus > 0:
        movable = [i for i in range(count - 1) if holding[i] < limit]
        mass, remaining = sum([portions[i] for i in movable]), surplus
        for i in movable:
            addition = min(limit - holding[i], max(1, remaining * portions[i] // mass), surplus)
            holding[i] = holding[i] + addition
            surplus = surplus - addition
    return np.array([limit] + holding)


def ragged_sizes(own_key, amount, total, limit, slope):
    if amount == 2:
        one = jax.random.randint(own_key, (), max(1, total - limit), min(limit, total - 1) + 1)
        return jnp.stack([one, total - one])
    lengths = jnp.asarray(length_profile(amount, total, limit, slope), jnp.int32)
    couples = (amount - 1) // 2
    source_of, sink = lengths[1:1 + 2 * couples:2], lengths[2:2 + 2 * couples:2]
    margin = jnp.minimum(source_of - 1, limit - sink)
    shifted = jax.random.randint(jax.random.fold_in(own_key, 1), (couples,), 0, 1 << 20) % (margin + 1)
    lengths = lengths.at[1:1 + 2 * couples:2].set(source_of - shifted).at[2:2 + 2 * couples:2].set(sink + shifted)
    return lengths[jax.random.permutation(jax.random.fold_in(own_key, 2), amount)]


def noise(key, extent, spread, reach, shards=(), kind=jnp.bfloat16):
    drawn = spread * jax.random.normal(key, extent, jnp.float32)
    if shards:
        drawn = drawn * block_scale(key, extent, shards, -0.22, 0.18)
    return jnp.clip(drawn, -reach, reach).astype(kind)


def setup_inputs(seed: int = 0) -> dict:
    streams_of = jax.random.split(jax.random.key(seed), 6)
    query_states = draw_query_states(jax.random.fold_in(streams_of[5], 71), 0)
    key_states = draw_key_states(jax.random.fold_in(streams_of[5], 71), 0)
    value_states = noise(streams_of[2], (TOKENS, KH * HD), 1.0, 6.0, ((0, 16), (1, 2)))
    out_weight = noise(streams_of[3], (QH * HD, D), (QH * HD) ** -0.5, 0.125, ((0, 2),))
    block_docs = jnp.searchsorted(jnp.cumsum(ragged_sizes(streams_of[4], DOCS, NBLK, MOST, 2)), jnp.arange(NBLK), side="right").astype(jnp.int32)
    return {"query_states": query_states, "key_states": key_states, "value_states": value_states, "out_weight": out_weight, "block_docs": block_docs}


def reference(query_states, key_states, value_states, out_weight, block_docs):
    group_size = QH // KH
    window = MOST * BLK
    score_scale = 1.0 / (HD ** 0.5)
    token_docs = jnp.repeat(block_docs, BLK, total_repeat_length=TOKENS)
    front = window - BLK
    key_padded = jnp.concatenate([jnp.zeros((front, KH * HD), key_states.dtype), key_states], axis=0)
    value_padded = jnp.concatenate([jnp.zeros((front, KH * HD), value_states.dtype), value_states], axis=0)
    docs_padded = jnp.concatenate([jnp.full((front,), -1, jnp.int32), token_docs.astype(jnp.int32)], axis=0)

    def one_block(block_index):
        start = (block_index * BLK).astype(jnp.int32)
        queries = lax.dynamic_slice_in_dim(query_states, start, BLK, 0).astype(jnp.float32).reshape(BLK, KH, group_size, HD)
        keys_here = lax.dynamic_slice_in_dim(key_padded, start, window, 0).astype(jnp.float32).reshape(window, KH, HD)
        values_here = lax.dynamic_slice_in_dim(value_padded, start, window, 0).astype(jnp.float32).reshape(window, KH, HD)
        query_docs = lax.dynamic_slice_in_dim(token_docs, start, BLK, 0)
        key_docs = lax.dynamic_slice_in_dim(docs_padded, start, window, 0)
        query_pos = start + jnp.arange(BLK, dtype=jnp.int32)
        key_pos = start - front + jnp.arange(window, dtype=jnp.int32)
        allowed = (query_docs[:, None] == key_docs[None, :]) & (key_pos[None, :] <= query_pos[:, None])
        scores = jnp.einsum("qgrd,kgd->grqk", queries, keys_here) * score_scale
        scores = jnp.where(allowed, scores, jnp.float32(-1e30))
        top = jnp.max(scores, axis=-1)
        weights = jnp.where(allowed, jnp.exp(scores - top[..., None]), jnp.float32(0.0))
        denominator = jnp.sum(weights, axis=-1)
        rounded = weights.astype(jnp.bfloat16).astype(jnp.float32)
        numerator = jnp.einsum("grqk,kgd->grqd", rounded, values_here)
        normalized = (numerator / denominator[..., None]).astype(jnp.bfloat16)
        return normalized.transpose(2, 0, 1, 3).reshape(BLK, QH * HD)

    attended = lax.map(one_block, jnp.arange(NBLK, dtype=jnp.int32)).reshape(TOKENS, QH * HD)
    group_width = QH * HD // N_HEAD

    def project(row_index):
        row_block = lax.dynamic_slice_in_dim(attended, (row_index * TOK_DEV).astype(jnp.int32), TOK_DEV, 0)
        summed = jnp.zeros((TOK_DEV, D), jnp.float32)
        for group in range(N_HEAD):
            partial_value = jnp.dot(row_block[:, group * group_width:(group + 1) * group_width], out_weight[group * group_width:(group + 1) * group_width], preferred_element_type=jnp.float32).astype(jnp.bfloat16)
            partial_value = lax.optimization_barrier(partial_value)
            summed = summed + partial_value.astype(jnp.float32)
        return summed.astype(jnp.bfloat16)

    return lax.map(project, jnp.arange(N_SEQ, dtype=jnp.int32)).reshape(TOKENS, D)
```

```python
import functools
import jax
import jax.numpy as jnp
from jax import lax
from jax.experimental import pallas as pl
from jax.experimental.pallas import tpu as pltpu
from jax.sharding import PartitionSpec as P

HD = 128
QH = 16
KH = 4
BLK = 128
DOC_BLK = 32
PARTS = 4
ROUND = 4
LOG2E = 1.4426950408889634
MIB = 1024 * 1024
VMEM = pl.BlockSpec(memory_space=pltpu.VMEM)
SMEM = pl.BlockSpec(memory_space=pltpu.SMEM)
ANY = pl.BlockSpec(memory_space=pl.ANY)


def cost(flops, bytes_accessed):
    return pl.CostEstimate(flops=flops, bytes_accessed=bytes_accessed, transcendentals=0)


def turned(value, axis, steps):
    count = lax.axis_size(axis)
    return lax.ppermute(value, axis, [(source, (source + steps) % count) for source in range(count)])


def stage_kernel(q_ref, w_ref, q_out, w_out, sems):
    groups, _, columns = w_out.shape
    group = lax.axis_index("head")
    copies = [pltpu.make_async_copy(q_ref, q_out, sems.at[groups])]
    for step in range(groups):
        target = lax.rem(group + step, groups)
        columns_of = pl.ds(pl.multiple_of(target * columns, 128), columns)
        copies.append(pltpu.make_async_copy(w_ref.at[:, columns_of], w_out.at[step], sems.at[step]))
    for copy in copies:
        copy.start()
    for copy in copies:
        copy.wait()


def stage(query_states, out_weight, groups):
    rows, columns = out_weight.shape
    return pl.pallas_call(
        stage_kernel,
        out_shape=(
            jax.ShapeDtypeStruct(query_states.shape, jnp.bfloat16),
            jax.ShapeDtypeStruct((groups, rows, columns // groups), jnp.bfloat16),
        ),
        in_specs=[ANY, ANY],
        out_specs=(VMEM, VMEM),
        scratch_shapes=[pltpu.SemaphoreType.DMA((groups + 1,))],
        compiler_params=pltpu.CompilerParams(vmem_limit_bytes=24 * MIB),
        cost_estimate=cost(0, 2 * out_weight.size * 2),
    )(query_states, out_weight)


def attend_kernel(blocks, kv_local, group_size, docs_ref, q_ref, *refs):
    kv_refs, w_ref, out_ref, part_ref = refs[:blocks], refs[blocks], refs[blocks + 1], refs[blocks + 2]
    width = kv_local * HD
    scale = jnp.float32(LOG2E / HD**0.5)
    position = lax.axis_index("seq")
    doc = docs_ref[position]
    near = [None]
    for offset in range(1, blocks):
        source = jnp.maximum(position - offset, 0)
        near.append((docs_ref[source] == doc) & (position >= offset))
    row = lax.broadcasted_iota(jnp.int32, (BLK, BLK), 0)
    column = lax.broadcasted_iota(jnp.int32, (BLK, BLK), 1)
    causal = jnp.concatenate([column <= row] * group_size, axis=0)
    for kv_head in range(kv_local):
        first = kv_head * group_size
        queries = jnp.concatenate(
            [q_ref[:, (first + g) * HD : (first + g + 1) * HD] for g in range(group_size)], axis=0
        )
        top = total = summed = None
        for start in range(0, blocks, ROUND):
            offsets = range(start, min(start + ROUND, blocks))
            scores = []
            for offset in offsets:
                keys = kv_refs[offset][:, kv_head * HD : (kv_head + 1) * HD]
                part = lax.dot_general(
                    queries, keys, (((1,), (1,)), ((), ())), preferred_element_type=jnp.float32
                )
                allowed = causal if offset == 0 else near[offset]
                scores.append(jnp.where(allowed, part, jnp.float32(-1e30)))
            largest = functools.reduce(jnp.maximum, scores)
            new_top = jnp.max(largest, axis=1, keepdims=True)
            if start:
                new_top = jnp.maximum(top, new_top)
            weights = [jnp.exp2((part - new_top) * scale) for part in scores]
            new_total = jnp.sum(functools.reduce(jnp.add, weights), axis=1, keepdims=True)
            values = jnp.concatenate(
                [
                    kv_refs[offset][:, width + kv_head * HD : width + (kv_head + 1) * HD]
                    for offset in offsets
                ],
                axis=0,
            )
            product = jnp.dot(
                jnp.concatenate([w.astype(jnp.bfloat16) for w in weights], axis=1),
                values,
                preferred_element_type=jnp.float32,
            )
            if start:
                factor = jnp.exp2((top - new_top) * scale)
                new_total = new_total + total * factor
                product = product + summed * factor
            top, total, summed = new_top, new_total, product
        attended = (summed / total).astype(jnp.bfloat16)
        for g in range(group_size):
            out_ref[:, (first + g) * HD : (first + g + 1) * HD] = attended[g * BLK : (g + 1) * BLK]
    width = part_ref.shape[1]
    part_ref[...] = jnp.dot(
        out_ref[...], w_ref[min(1, w_ref.shape[0] - 1), :, :width], preferred_element_type=jnp.float32
    ).astype(jnp.bfloat16)


def attend(docs, query_states, kv_blocks, weights, kv_local, group_size, width):
    return pl.pallas_call(
        functools.partial(attend_kernel, len(kv_blocks), kv_local, group_size),
        out_shape=(
            jax.ShapeDtypeStruct(query_states.shape, jnp.bfloat16),
            jax.ShapeDtypeStruct((BLK, width), jnp.bfloat16),
        ),
        in_specs=[SMEM] + [VMEM] * (2 + len(kv_blocks)),
        out_specs=(VMEM, VMEM),
        compiler_params=pltpu.CompilerParams(vmem_limit_bytes=32 * MIB),
        cost_estimate=cost(600_000_000, 2_000_000),
    )(docs, query_states, *kv_blocks, weights)


def project_kernel(step, width, a_ref, w_ref, *out_refs):
    first = w_ref.shape[2] - width * len(out_refs)
    for i, out_ref in enumerate(out_refs):
        out_ref[...] = jnp.dot(
            a_ref[...],
            w_ref[step, :, first + i * width : first + (i + 1) * width],
            preferred_element_type=jnp.float32,
        ).astype(jnp.bfloat16)


def project(attended, weights, step, width, count):
    return pl.pallas_call(
        functools.partial(project_kernel, step, width),
        out_shape=[jax.ShapeDtypeStruct((BLK, width), jnp.bfloat16)] * count,
        in_specs=[VMEM, VMEM],
        out_specs=[VMEM] * count,
        compiler_params=pltpu.CompilerParams(vmem_limit_bytes=24 * MIB),
        cost_estimate=cost(2 * BLK * width * count * attended.shape[1], 1_000_000),
    )(attended, weights)


def local(query_states, key_states, value_states, out_weight, block_docs):
    tokens_here = query_states.shape[0]
    kv_local = key_states.shape[1] // HD
    group_size = QH // KH
    block_count = block_docs.shape[0]
    groups = lax.axis_size("head")
    assert tokens_here == BLK and block_count == lax.axis_size("seq")
    reach = min(DOC_BLK, block_count // 4) - 1

    kv = jnp.concatenate([key_states, value_states], axis=1)
    if reach <= 3:
        kv_blocks = [kv] + [turned(kv, "seq", offset) for offset in range(reach, 0, -1)][::-1]
    else:
        kv_blocks = [kv]
        while len(kv_blocks) < reach + 1:
            have = len(kv_blocks)
            send = min(have, reach + 1 - have)
            arrived = turned(jnp.stack(kv_blocks[:send]), "seq", have)
            kv_blocks = kv_blocks + [arrived[i] for i in range(send)]

    queries, weights = stage(query_states, out_weight, groups)
    width = out_weight.shape[1] // groups // PARTS
    attended, first = attend(block_docs, queries, kv_blocks, weights, kv_local, group_size, width)

    received = []
    for step in range(1, groups):
        if step == 1:
            row = [first] + list(project(attended, weights, 1, width, PARTS - 1))
        else:
            row = list(project(attended, weights, step, width, PARTS))
        received.append([turned(partial, "head", step) for partial in row])
    mine = project(attended, weights, 0, width, PARTS)
    outs = []
    for i in range(PARTS):
        total = mine[i].astype(jnp.float32)
        for row in received:
            total = total + row[i].astype(jnp.float32)
        outs.append(total.astype(jnp.bfloat16))
    return jnp.concatenate(outs, axis=1)


def solution(mesh):
    return jax.shard_map(
        local,
        mesh=mesh,
        in_specs=(P("seq", "head"), P("seq", "head"), P("seq", "head"), P("head", None), P()),
        out_specs=P("seq", "head"),
        check_vma=False,
    )
```

```python
import functools
import jax
import jax.numpy as jnp
from jax import lax
from jax.experimental import pallas as pl
from jax.experimental.pallas import tpu as pltpu
from jax.sharding import PartitionSpec as P

HD = 128
QH = 16
KH = 4
BLK = 128
DOC_BLK = 32
PARTS = 4
ROUND = 4
LOG2E = 1.4426950408889634
MIB = 1024 * 1024
FAR = -1e30
VMEM = pl.BlockSpec(memory_space=pltpu.VMEM)
SMEM = pl.BlockSpec(memory_space=pltpu.SMEM)
HBM = pl.BlockSpec(memory_space=pltpu.HBM)
RINGS = (
    (2, 0, 3, 1, 5, 8, 7, 9, 10, 4, 6, 14, 13, 12, 15, 11),
    (1, 3, 4, 6, 0, 7, 8, 2, 5, 11, 12, 13, 14, 9, 15, 10),
    (1, 4, 3, 5, 6, 0, 2, 10, 9, 12, 11, 7, 8, 15, 13, 14),
)


def cost(flops, bytes_accessed):
    return pl.CostEstimate(flops=flops, bytes_accessed=bytes_accessed, transcendentals=0)


def turned(value, axis, steps):
    count = lax.axis_size(axis)
    return lax.ppermute(value, axis, [(source, (source + steps) % count) for source in range(count)])


def ring_table():
    gaps, carrier, seen = [0] * len(RINGS), 0, set()
    for at, ring in enumerate(RINGS):
        for source, target in enumerate(ring):
            gap = target - source
            wanted = gap == 2 or gap == (3 if source % 2 else 1)
            if wanted and (source, target) not in seen:
                seen.add((source, target))
                gaps[at] |= gap << 2 * target
                if gap == 2:
                    carrier |= at << 2 * target
    assert len(seen) == 5 * len(RINGS[0]) // 2 - 12
    return gaps, carrier


def pick(packed, position):
    signed = packed - (1 << 32) if packed >= 1 << 31 else packed
    return lax.shift_right_logical(jnp.int32(signed), 2 * position) & 3


def hold_kernel(kv_in, kv_out):
    pass


def hold(kv):
    return pl.pallas_call(
        hold_kernel,
        out_shape=jax.ShapeDtypeStruct(kv.shape, kv.dtype),
        in_specs=[VMEM],
        out_specs=VMEM,
        input_output_aliases={0: 0},
        compiler_params=pltpu.CompilerParams(vmem_limit_bytes=2 * MIB),
        cost_estimate=cost(10_000_000_000, 0),
    )(kv)


def choose_kernel(carrier, *refs):
    *arrived_refs, _, out_ref = refs
    holder = pick(carrier, lax.axis_index("seq"))
    for at, ref in enumerate(arrived_refs):

        @pl.when(holder == at)
        def _():
            out_ref[...] = ref[...]


def choose(carrier, arrived, after):
    return pl.pallas_call(
        functools.partial(choose_kernel, carrier),
        out_shape=jax.ShapeDtypeStruct(arrived[0].shape, arrived[0].dtype),
        in_specs=[VMEM] * (len(arrived) + 1),
        out_specs=VMEM,
        compiler_params=pltpu.CompilerParams(vmem_limit_bytes=4 * MIB),
        cost_estimate=cost(0, 300_000),
    )(*arrived, after)


def opening_kernel(gaps, kv_local, group_size, docs_ref, q_ref, kv_ref, *refs):
    *state_refs, bias_ref = refs
    position = lax.axis_index("seq")
    doc = docs_ref[position]
    for at, gap in enumerate(gaps):
        gap = gap(position)
        source = jnp.maximum(position - gap, 0)
        near = (docs_ref[source] == doc) & (position >= gap) & (gap > 0)
        bias_ref[at] = jnp.full(bias_ref.shape[1:], jnp.where(near, 0.0, FAR), jnp.float32)
    attend_kernel(1, True, kv_local, group_size, False, False, q_ref, kv_ref, *state_refs)


def opening(docs, queries, kv, weights, gaps, kv_local, group_size):
    rows = group_size * BLK
    state = [jax.ShapeDtypeStruct((kv_local, n, rows), jnp.float32) for n in (1, 1, HD)]
    bias = jax.ShapeDtypeStruct((len(gaps), 1, rows), jnp.float32)
    *state, bias = pl.pallas_call(
        functools.partial(opening_kernel, gaps, kv_local, group_size),
        out_shape=[*state, bias],
        in_specs=[SMEM, VMEM, VMEM],
        out_specs=[VMEM] * 4,
        compiler_params=pltpu.CompilerParams(vmem_limit_bytes=20 * MIB),
        cost_estimate=cost(500_000_000, 1_000_000),
    )(docs, queries, kv)
    return state, bias


def heads_of(kv_head, group_size):
    return range(kv_head * group_size, (kv_head + 1) * group_size)


def attend_kernel(blocks, own, kv_local, group_size, resume, finish, q_ref, *refs):
    refs = list(refs)
    kv_refs = [refs.pop(0) for _ in range(blocks)]
    bias_refs = [refs.pop(0) for _ in range(blocks - own)]
    state_in = [refs.pop(0) for _ in range(3)] if resume else None
    w_ref = refs.pop(0) if finish else None
    width = kv_local * HD
    scale = jnp.float32(LOG2E / HD**0.5)
    if own:
        row = lax.broadcasted_iota(jnp.int32, (BLK, BLK), 0)
        column = lax.broadcasted_iota(jnp.int32, (BLK, BLK), 1)
        causal = jnp.concatenate([row <= column] * group_size, axis=1)
    states = [[ref[kv_head] for ref in state_in] if resume else None for kv_head in range(kv_local)]
    queries = [
        jnp.concatenate([q_ref[:, h * HD : (h + 1) * HD] for h in heads_of(kv_head, group_size)], axis=0)
        for kv_head in range(kv_local)
    ]
    for start in range(0, blocks, ROUND):
        picked = range(start, min(start + ROUND, blocks))
        scores = [
            [
                lax.dot_general(
                    kv_refs[at][:, kv_head * HD : (kv_head + 1) * HD],
                    queries[kv_head],
                    (((1,), (1,)), ((), ())),
                    preferred_element_type=jnp.float32,
                )
                for at in picked
            ]
            for kv_head in range(kv_local)
        ]
        for kv_head in range(kv_local):
            parts = [
                jnp.where(causal, part, FAR) if own and at == 0 else part + bias_refs[at - own][...]
                for at, part in zip(picked, scores[kv_head])
            ]
            state = states[kv_head]
            top = jnp.max(functools.reduce(jnp.maximum, parts), axis=0, keepdims=True)
            if state:
                top = jnp.maximum(state[0], top)
            weights = [jnp.exp2((part - top) * scale) for part in parts]
            total = jnp.sum(functools.reduce(jnp.add, weights), axis=0, keepdims=True)
            values = [
                kv_refs[at][:, width + kv_head * HD : width + (kv_head + 1) * HD] for at in picked
            ]
            summed = lax.dot_general(
                jnp.concatenate(values, axis=0),
                jnp.concatenate([w.astype(jnp.bfloat16) for w in weights], axis=0),
                (((0,), (0,)), ((), ())),
                preferred_element_type=jnp.float32,
            )
            if state:
                factor = jnp.exp2((state[0] - top) * scale)
                total = total + state[1] * factor
                summed = summed + state[2] * factor
            states[kv_head] = [top, total, summed]
    for kv_head, state in enumerate(states):
        if finish:
            attended = state[2] * (1.0 / state[1])
            for g, h in enumerate(heads_of(kv_head, group_size)):
                turned_back = attended[:, g * BLK : (g + 1) * BLK].T
                refs[0][:, h * HD : (h + 1) * HD] = turned_back.astype(jnp.bfloat16)
        else:
            for ref, value in zip(refs, state):
                ref[kv_head] = value
    if finish:
        out_ref, part_ref = refs
        part_ref[...] = project_part(out_ref, w_ref, 1, 0, part_ref.shape[1])


def first_column(columns, step):
    groups = lax.axis_size("head")
    target = lax.rem(lax.axis_index("head") + step, groups)
    return pl.multiple_of(target * (columns // groups), 128)


def attend(queries, kv_blocks, biases, kv_local, group_size, state, weights=None, width=0):
    rows = group_size * BLK
    if width:
        out_shape = [
            jax.ShapeDtypeStruct(queries.shape, jnp.bfloat16),
            jax.ShapeDtypeStruct((BLK, width), jnp.bfloat16),
        ]
    else:
        out_shape = [jax.ShapeDtypeStruct((kv_local, n, rows), jnp.float32) for n in (1, 1, HD)]
    operands = [queries, *kv_blocks, *biases, *state] + ([weights] if width else [])
    blocks = len(kv_blocks)
    return pl.pallas_call(
        functools.partial(
            attend_kernel, blocks, len(biases) < blocks, kv_local, group_size, bool(state), bool(width)
        ),
        out_shape=out_shape,
        in_specs=[VMEM] * len(operands),
        out_specs=[VMEM] * len(out_shape),
        compiler_params=pltpu.CompilerParams(vmem_limit_bytes=20 * MIB),
        cost_estimate=cost(1_000_000_000, 2_000_000),
    )(*operands)


def project_part(a_ref, w_ref, step, part, width):
    begin = pl.multiple_of(first_column(w_ref.shape[1], step) + part * width, 128)
    return jnp.dot(
        a_ref[...], w_ref[:, pl.ds(begin, width)], preferred_element_type=jnp.float32
    ).astype(jnp.bfloat16)


def project_kernel(step, parts, a_ref, w_ref, *out_refs):
    for part, out_ref in zip(parts, out_refs):
        out_ref[...] = project_part(a_ref, w_ref, step, part, out_ref.shape[1])


def project(attended, weights, step, parts, width):
    return pl.pallas_call(
        functools.partial(project_kernel, step, parts),
        out_shape=[jax.ShapeDtypeStruct((BLK, width), jnp.bfloat16)] * len(parts),
        in_specs=[VMEM, VMEM],
        out_specs=[VMEM] * len(parts),
        compiler_params=pltpu.CompilerParams(vmem_limit_bytes=20 * MIB),
        cost_estimate=cost(2 * BLK * width * len(parts) * attended.shape[1], 1_000_000),
    )(attended, weights)


def mask_kernel(docs_ref, bias_ref):
    position = lax.axis_index("seq")
    doc = docs_ref[position]
    for at in range(bias_ref.shape[0]):
        near = (docs_ref[jnp.maximum(position - at - 1, 0)] == doc) & (position > at)
        bias_ref[at] = jnp.full(bias_ref.shape[1:], jnp.where(near, 0.0, FAR), jnp.float32)


def mask(docs, reach, rows):
    return pl.pallas_call(
        mask_kernel,
        out_shape=jax.ShapeDtypeStruct((reach, 1, rows), jnp.float32),
        in_specs=[SMEM],
        out_specs=VMEM,
    )(docs)


def side_by_side(left, right):
    low = jnp.array(-jnp.inf, left.dtype)
    first = lax.pad(left, low, ((0, 0, 0), (0, right.shape[1], 0)))
    return jnp.maximum(first, lax.pad(right, low, ((0, 0, 0), (left.shape[1], 0, 0))))


def local(query_states, key_states, value_states, out_weight, block_docs):
    tokens_here = query_states.shape[0]
    kv_local = key_states.shape[1] // HD
    group_size = QH // KH
    count = lax.axis_size("seq")
    groups = lax.axis_size("head")
    assert tokens_here == BLK and block_docs.shape[0] == count
    reach = min(DOC_BLK, count // 4) - 1
    width = out_weight.shape[1] // groups // PARTS
    sizes = (kv_local, group_size)

    kv = hold(side_by_side(key_states, value_states))
    if reach == 3 and count == len(RINGS[0]):
        packed, carrier = ring_table()
        arrived = [lax.ppermute(kv, "seq", list(enumerate(ring))) for ring in RINGS]
        gaps = [functools.partial(pick, word) for word in packed]
        gaps.append(lambda position: 1 + 2 * (position & 1))
        state, bias = opening(block_docs, query_states, kv, out_weight, gaps, *sizes)
        second = choose(carrier, arrived, state[0])
        late = lax.ppermute(second, "seq", [(i, i ^ 1) for i in range(count)])
        biases = [bias[at] for at in range(len(gaps))]
        state = attend(query_states, arrived, biases[:-1], *sizes, state)
        attended, first = attend(query_states, [late], biases[-1:], *sizes, state, out_weight, width)
    else:
        blocks = [kv]
        while len(blocks) < reach + 1:
            have = len(blocks)
            send = min(have, reach + 1 - have)
            passed = turned(jnp.stack(blocks[:send]), "seq", have)
            blocks = blocks + [passed[i] for i in range(send)]
        bias = mask(block_docs, reach, group_size * BLK)
        biases = [bias[at] for at in range(reach)]
        attended, first = attend(query_states, blocks, biases, *sizes, (), out_weight, width)

    received = []
    for step in range(1, groups):
        if step == 1:
            row = [first] + list(project(attended, out_weight, 1, range(1, PARTS), width))
        else:
            row = project(attended, out_weight, step, range(PARTS), width)
        received.append([turned(partial, "head", step) for partial in row])
    mine = project(attended, out_weight, 0, range(PARTS), width)
    outs = []
    for i in range(PARTS):
        total = mine[i].astype(jnp.float32)
        for row in received:
            total = total + row[i].astype(jnp.float32)
        outs.append(total.astype(jnp.bfloat16))
    return jnp.concatenate(outs, axis=1)


def solution(mesh):
    return jax.shard_map(
        local,
        mesh=mesh,
        in_specs=(P("seq", "head"), P("seq", "head"), P("seq", "head"), P("head", None), P()),
        out_specs=P("seq", "head"),
        check_vma=False,
    )
```

```python
import functools
import jax
import jax.numpy as jnp
from jax import lax
from jax.experimental import pallas as pl
from jax.experimental.pallas import tpu as pltpu
from jax.sharding import PartitionSpec as P

HD = 128
QH = 16
KH = 4
BLK = 128
DOC_BLK = 32
PARTS = 4
ROUND = 4
LOG2E = 1.4426950408889634
MIB = 1024 * 1024
FAR = -1e30
VMEM = pl.BlockSpec(memory_space=pltpu.VMEM)
SMEM = pl.BlockSpec(memory_space=pltpu.SMEM)
HBM = pl.BlockSpec(memory_space=pltpu.HBM)
RINGS = (
    (1, 4, 3, 6, 5, 0, 2, 10, 9, 12, 7, 14, 13, 8, 15, 11),
    (1, 0, 3, 5, 6, 7, 8, 2, 10, 4, 11, 13, 14, 9, 15, 12),
    (2, 3, 4, 0, 1, 8, 7, 9, 5, 11, 12, 6, 13, 15, 10, 14),
)


def cost(flops, bytes_accessed):
    return pl.CostEstimate(flops=flops, bytes_accessed=bytes_accessed, transcendentals=0)


def turned(value, axis, steps):
    count = lax.axis_size(axis)
    return lax.ppermute(value, axis, [(source, (source + steps) % count) for source in range(count)])


def ring_table():
    gaps, carrier, seen = [0] * len(RINGS), 0, set()
    for at, ring in enumerate(RINGS):
        for source, target in enumerate(ring):
            gap = target - source
            wanted = gap == 2 or gap == (3 if source % 2 else 1)
            if wanted and (source, target) not in seen:
                seen.add((source, target))
                gaps[at] |= gap << 2 * target
                if gap == 2:
                    carrier |= (at - 1) << 2 * target
    assert len(seen) == 5 * len(RINGS[0]) // 2 - 12
    return gaps, carrier


def pick(packed, position):
    signed = packed - (1 << 32) if packed >= 1 << 31 else packed
    return lax.shift_right_logical(jnp.int32(signed), 2 * position) & 3


def hold_kernel(kv_in, kv_out):
    pass


def hold(kv):
    return pl.pallas_call(
        hold_kernel,
        out_shape=jax.ShapeDtypeStruct(kv.shape, kv.dtype),
        in_specs=[VMEM],
        out_specs=VMEM,
        input_output_aliases={0: 0},
        compiler_params=pltpu.CompilerParams(vmem_limit_bytes=2 * MIB),
        cost_estimate=cost(10_000_000_000, 0),
    )(kv)


def choose_kernel(carrier, *refs):
    *arrived_refs, _, out_ref = refs
    holder = pick(carrier, lax.axis_index("seq"))
    for at, ref in enumerate(arrived_refs):

        @pl.when(holder == at)
        def _():
            out_ref[...] = ref[...]


def choose(carrier, arrived, after):
    return pl.pallas_call(
        functools.partial(choose_kernel, carrier),
        out_shape=jax.ShapeDtypeStruct(arrived[0].shape, arrived[0].dtype),
        in_specs=[VMEM] * (len(arrived) + 1),
        out_specs=VMEM,
        compiler_params=pltpu.CompilerParams(vmem_limit_bytes=4 * MIB),
        cost_estimate=cost(0, 300_000),
    )(*arrived, after)


def opening_kernel(gaps, kv_local, group_size, docs_ref, q_ref, kv_ref, *refs):
    *state_refs, bias_ref, kv_out = refs
    kv_out[...] = kv_ref[...]
    position = lax.axis_index("seq")
    doc = docs_ref[position]
    for at, gap in enumerate(gaps):
        gap = gap(position)
        source = jnp.maximum(position - gap, 0)
        near = (docs_ref[source] == doc) & (position >= gap) & (gap > 0)
        bias_ref[at] = jnp.full(bias_ref.shape[1:], jnp.where(near, 0.0, FAR), jnp.float32)
    attend_kernel(1, True, kv_local, group_size, False, False, q_ref, kv_ref, *state_refs)


def opening(docs, queries, kv, weights, gaps, kv_local, group_size):
    rows = group_size * BLK
    state = [jax.ShapeDtypeStruct((kv_local, n, rows), jnp.float32) for n in (1, 1, HD)]
    bias = jax.ShapeDtypeStruct((len(gaps), 1, rows), jnp.float32)
    *state, bias, kv = pl.pallas_call(
        functools.partial(opening_kernel, gaps, kv_local, group_size),
        out_shape=[*state, bias, jax.ShapeDtypeStruct(kv.shape, kv.dtype)],
        in_specs=[SMEM, VMEM, VMEM],
        out_specs=[VMEM] * 5,
        compiler_params=pltpu.CompilerParams(vmem_limit_bytes=20 * MIB),
        cost_estimate=cost(500_000_000, 1_000_000),
    )(docs, queries, kv)
    return state, bias, kv


def heads_of(kv_head, group_size):
    return range(kv_head * group_size, (kv_head + 1) * group_size)


def attend_kernel(blocks, own, kv_local, group_size, resume, finish, q_ref, *refs):
    refs = list(refs)
    kv_refs = [refs.pop(0) for _ in range(blocks)]
    bias_refs = [refs.pop(0) for _ in range(blocks - own)]
    state_in = [refs.pop(0) for _ in range(3)] if resume else None
    w_ref = refs.pop(0) if finish else None
    width = kv_local * HD
    scale = jnp.float32(LOG2E / HD**0.5)
    if own:
        row = lax.broadcasted_iota(jnp.int32, (BLK, BLK), 0)
        column = lax.broadcasted_iota(jnp.int32, (BLK, BLK), 1)
        causal = jnp.concatenate([row <= column] * group_size, axis=1)
    states = [[ref[kv_head] for ref in state_in] if resume else None for kv_head in range(kv_local)]
    queries = [
        jnp.concatenate([q_ref[:, h * HD : (h + 1) * HD] for h in heads_of(kv_head, group_size)], axis=0)
        for kv_head in range(kv_local)
    ]
    for start in range(0, blocks, ROUND):
        picked = range(start, min(start + ROUND, blocks))
        scores = [
            [
                lax.dot_general(
                    kv_refs[at][:, kv_head * HD : (kv_head + 1) * HD],
                    queries[kv_head],
                    (((1,), (1,)), ((), ())),
                    preferred_element_type=jnp.float32,
                )
                for at in picked
            ]
            for kv_head in range(kv_local)
        ]
        for kv_head in range(kv_local):
            parts = [
                jnp.where(causal, part, FAR) if own and at == 0 else part + bias_refs[at - own][...]
                for at, part in zip(picked, scores[kv_head])
            ]
            state = states[kv_head]
            top = jnp.max(functools.reduce(jnp.maximum, parts), axis=0, keepdims=True)
            if state:
                top = jnp.maximum(state[0], top)
            weights = [jnp.exp2((part - top) * scale) for part in parts]
            total = jnp.sum(functools.reduce(jnp.add, weights), axis=0, keepdims=True)
            values = [
                kv_refs[at][:, width + kv_head * HD : width + (kv_head + 1) * HD] for at in picked
            ]
            summed = lax.dot_general(
                jnp.concatenate(values, axis=0),
                jnp.concatenate([w.astype(jnp.bfloat16) for w in weights], axis=0),
                (((0,), (0,)), ((), ())),
                preferred_element_type=jnp.float32,
            )
            if state:
                factor = jnp.exp2((state[0] - top) * scale)
                total = total + state[1] * factor
                summed = summed + state[2] * factor
            states[kv_head] = [top, total, summed]
    for kv_head, state in enumerate(states):
        if finish:
            attended = state[2] * (1.0 / state[1])
            for g, h in enumerate(heads_of(kv_head, group_size)):
                turned_back = attended[:, g * BLK : (g + 1) * BLK].T
                refs[0][:, h * HD : (h + 1) * HD] = turned_back.astype(jnp.bfloat16)
        else:
            for ref, value in zip(refs, state):
                ref[kv_head] = value
    if finish:
        out_ref, part_ref = refs
        part_ref[...] = project_part(out_ref, w_ref, 1, PARTS - 1, part_ref.shape[1])


def first_column(columns, step):
    groups = lax.axis_size("head")
    target = lax.rem(lax.axis_index("head") + step, groups)
    return pl.multiple_of(target * (columns // groups), 128)


def attend(queries, kv_blocks, biases, kv_local, group_size, state, weights=None, width=0):
    rows = group_size * BLK
    if width:
        out_shape = [
            jax.ShapeDtypeStruct(queries.shape, jnp.bfloat16),
            jax.ShapeDtypeStruct((BLK, width), jnp.bfloat16),
        ]
    else:
        out_shape = [jax.ShapeDtypeStruct((kv_local, n, rows), jnp.float32) for n in (1, 1, HD)]
    operands = [queries, *kv_blocks, *biases, *state] + ([weights] if width else [])
    blocks = len(kv_blocks)
    return pl.pallas_call(
        functools.partial(
            attend_kernel, blocks, len(biases) < blocks, kv_local, group_size, bool(state), bool(width)
        ),
        out_shape=out_shape,
        in_specs=[VMEM] * len(operands),
        out_specs=[VMEM] * len(out_shape),
        compiler_params=pltpu.CompilerParams(vmem_limit_bytes=20 * MIB),
        cost_estimate=cost(1_000_000_000, 2_000_000),
    )(*operands)


def project_part(a_ref, w_ref, step, part, width):
    begin = pl.multiple_of(first_column(w_ref.shape[1], step) + part * width, 128)
    return jnp.dot(
        a_ref[...], w_ref[:, pl.ds(begin, width)], preferred_element_type=jnp.float32
    ).astype(jnp.bfloat16)


def project_kernel(step, parts, a_ref, w_ref, *out_refs):
    for part, out_ref in zip(parts, out_refs):
        out_ref[...] = project_part(a_ref, w_ref, step, part, out_ref.shape[1])


def project(attended, weights, step, parts, width):
    return pl.pallas_call(
        functools.partial(project_kernel, step, parts),
        out_shape=[jax.ShapeDtypeStruct((BLK, width), jnp.bfloat16)] * len(parts),
        in_specs=[VMEM, VMEM],
        out_specs=[VMEM] * len(parts),
        compiler_params=pltpu.CompilerParams(vmem_limit_bytes=20 * MIB),
        cost_estimate=cost(2 * BLK * width * len(parts) * attended.shape[1], 1_000_000),
    )(attended, weights)


def close_kernel(parts, each, resume, *refs):
    refs = list(refs)
    mine_refs = [refs.pop(0) for _ in parts]
    other_refs = [[refs.pop(0) for _ in range(each)] for _ in parts]
    if resume:
        refs.pop(0)
    out_ref, sums, sems = refs
    width = mine_refs[0].shape[1]
    copies = []
    for at, part in enumerate(parts):
        total = mine_refs[at][...].astype(jnp.float32)
        for ref in other_refs[at]:
            total = total + ref[...].astype(jnp.float32)
        sums[at] = total.astype(sums.dtype)
        columns = slice(part * width, (part + 1) * width)
        copies.append(pltpu.make_async_copy(sums.at[at], out_ref.at[:, columns], sems.at[at]))
        copies[-1].start()
    for copy in copies:
        copy.wait()


def close(parts, mine, received, columns, out=None):
    rows, width = mine[0].shape
    others = [row[part] for part in parts for row in received]
    operands = [mine[part] for part in parts] + others + ([] if out is None else [out])
    return pl.pallas_call(
        functools.partial(close_kernel, tuple(parts), len(received), out is not None),
        out_shape=jax.ShapeDtypeStruct((rows, columns), mine[0].dtype),
        in_specs=[VMEM] * (len(parts) + len(others)) + ([] if out is None else [HBM]),
        out_specs=HBM,
        scratch_shapes=[
            pltpu.VMEM((len(parts), rows, width), mine[0].dtype),
            pltpu.SemaphoreType.DMA((len(parts),)),
        ],
        input_output_aliases={} if out is None else {len(operands) - 1: 0},
        compiler_params=pltpu.CompilerParams(vmem_limit_bytes=8 * MIB),
        cost_estimate=cost(1_000_000, 1_000_000),
    )(*operands)


def mask_kernel(docs_ref, bias_ref):
    position = lax.axis_index("seq")
    doc = docs_ref[position]
    for at in range(bias_ref.shape[0]):
        near = (docs_ref[jnp.maximum(position - at - 1, 0)] == doc) & (position > at)
        bias_ref[at] = jnp.full(bias_ref.shape[1:], jnp.where(near, 0.0, FAR), jnp.float32)


def mask(docs, reach, rows):
    return pl.pallas_call(
        mask_kernel,
        out_shape=jax.ShapeDtypeStruct((reach, 1, rows), jnp.float32),
        in_specs=[SMEM],
        out_specs=VMEM,
    )(docs)


def side_by_side(left, right):
    low = jnp.array(-jnp.inf, left.dtype)
    first = lax.pad(left, low, ((0, 0, 0), (0, right.shape[1], 0)))
    return jnp.maximum(first, lax.pad(right, low, ((0, 0, 0), (left.shape[1], 0, 0))))


def local(query_states, key_states, value_states, out_weight, block_docs):
    tokens_here = query_states.shape[0]
    kv_local = key_states.shape[1] // HD
    group_size = QH // KH
    count = lax.axis_size("seq")
    groups = lax.axis_size("head")
    assert tokens_here == BLK and block_docs.shape[0] == count
    reach = min(DOC_BLK, count // 4) - 1
    width = out_weight.shape[1] // groups // PARTS
    sizes = (kv_local, group_size)

    kv = hold(side_by_side(key_states, value_states))
    if reach == 3 and count == len(RINGS[0]):
        packed, carrier = ring_table()
        arrived = [lax.ppermute(kv, "seq", list(enumerate(ring))) for ring in RINGS[1:]]
        gaps = [functools.partial(pick, word) for word in packed]
        gaps.append(lambda position: 1 + 2 * (position & 1))
        state, bias, kv = opening(block_docs, query_states, kv, out_weight, gaps, *sizes)
        arrived = [lax.ppermute(kv, "seq", list(enumerate(RINGS[0])))] + arrived
        second = choose(carrier, arrived[1:], state[0])
        late = lax.ppermute(second, "seq", [(i, i ^ 1) for i in range(count)])
        biases = [bias[at] for at in range(len(gaps))]
        state = attend(query_states, arrived[1:], biases[1:3], *sizes, state)
        attended, last = attend(
            query_states, [arrived[0], late], [biases[0], biases[3]], *sizes, state, out_weight, width
        )
    else:
        blocks = [kv]
        while len(blocks) < reach + 1:
            have = len(blocks)
            send = min(have, reach + 1 - have)
            passed = turned(jnp.stack(blocks[:send]), "seq", have)
            blocks = blocks + [passed[i] for i in range(send)]
        bias = mask(block_docs, reach, group_size * BLK)
        biases = [bias[at] for at in range(reach)]
        attended, last = attend(query_states, blocks, biases, *sizes, (), out_weight, width)

    received = []
    for step in range(1, groups):
        if step == 1:
            row = list(project(attended, out_weight, 1, range(PARTS - 1), width)) + [last]
        else:
            row = project(attended, out_weight, step, range(PARTS), width)
        received.append([turned(partial, "head", step) for partial in row])
    mine = project(attended, out_weight, 0, range(PARTS), width)
    columns = out_weight.shape[1] // groups
    out = close([PARTS - 1, *range(PARTS - 2)], mine, received, columns)
    return close([PARTS - 2], mine, received, columns, out)


def solution(mesh):
    return jax.shard_map(
        local,
        mesh=mesh,
        in_specs=(P("seq", "head"), P("seq", "head"), P("seq", "head"), P("head", None), P()),
        out_specs=P("seq", "head"),
        check_vma=False,
    )
```

```python
import functools
import jax
import jax.numpy as jnp
from jax import lax
from jax.experimental import pallas as pl
from jax.experimental.pallas import tpu as pltpu
from jax.sharding import PartitionSpec as P

HD = 128
QH = 16
KH = 4
BLK = 128
DOC_BLK = 32
PARTS = (2, 2, 2, 2)
ROUND = 4
LOG2E = 1.4426950408889634
MIB = 1024 * 1024
FAR = -1e30
VMEM = pl.BlockSpec(memory_space=pltpu.VMEM)
SMEM = pl.BlockSpec(memory_space=pltpu.SMEM)
HBM = pl.BlockSpec(memory_space=pltpu.HBM)
RINGS = (
    (1, 4, 3, 6, 5, 0, 2, 10, 9, 12, 7, 14, 13, 8, 15, 11),
    (1, 0, 3, 5, 6, 7, 8, 2, 10, 4, 11, 13, 14, 9, 15, 12),
    (2, 3, 4, 0, 1, 8, 7, 9, 5, 11, 12, 6, 13, 15, 10, 14),
)


def cost(flops, bytes_accessed):
    return pl.CostEstimate(flops=flops, bytes_accessed=bytes_accessed, transcendentals=0)


def turned(value, axis, steps):
    count = lax.axis_size(axis)
    return lax.ppermute(value, axis, [(source, (source + steps) % count) for source in range(count)])


def ring_table():
    gaps, carrier, seen = [0] * len(RINGS), 0, set()
    for at, ring in enumerate(RINGS):
        for source, target in enumerate(ring):
            gap = target - source
            wanted = gap == 2 or gap == (3 if source % 2 else 1)
            if wanted and (source, target) not in seen:
                seen.add((source, target))
                gaps[at] |= gap << 2 * target
                if gap == 2:
                    carrier |= (at - 1) << 2 * target
    assert len(seen) == 5 * len(RINGS[0]) // 2 - 12
    return gaps, carrier


def pick(packed, position):
    signed = packed - (1 << 32) if packed >= 1 << 31 else packed
    return lax.shift_right_logical(jnp.int32(signed), 2 * position) & 3


def hold_kernel(kv_in, kv_out):
    pass


def hold(kv):
    return pl.pallas_call(
        hold_kernel,
        out_shape=jax.ShapeDtypeStruct(kv.shape, kv.dtype),
        in_specs=[VMEM],
        out_specs=VMEM,
        input_output_aliases={0: 0},
        compiler_params=pltpu.CompilerParams(vmem_limit_bytes=2 * MIB),
        cost_estimate=cost(6_000_000_000, 0),
    )(kv)


def choose_kernel(carrier, *refs):
    *arrived_refs, _, out_ref = refs
    holder = pick(carrier, lax.axis_index("seq"))
    for at, ref in enumerate(arrived_refs):

        @pl.when(holder == at)
        def _():
            out_ref[...] = ref[...]


def choose(carrier, arrived, after):
    return pl.pallas_call(
        functools.partial(choose_kernel, carrier),
        out_shape=jax.ShapeDtypeStruct(arrived[0].shape, arrived[0].dtype),
        in_specs=[VMEM] * (len(arrived) + 1),
        out_specs=VMEM,
        compiler_params=pltpu.CompilerParams(vmem_limit_bytes=4 * MIB),
        cost_estimate=cost(0, 300_000),
    )(*arrived, after)


def opening_kernel(gaps, kv_local, group_size, docs_ref, q_ref, kv_ref, *refs):
    *state_refs, bias_ref, kv_out = refs
    kv_out[...] = kv_ref[...]
    position = lax.axis_index("seq")
    doc = docs_ref[position]
    for at, gap in enumerate(gaps):
        gap = gap(position)
        source = jnp.maximum(position - gap, 0)
        near = (docs_ref[source] == doc) & (position >= gap) & (gap > 0)
        bias_ref[at] = jnp.full(bias_ref.shape[1:], jnp.where(near, 0.0, FAR), jnp.float32)
    attend_kernel(1, True, kv_local, group_size, False, False, q_ref, kv_ref, *state_refs)


def opening(docs, queries, kv, weights, gaps, kv_local, group_size):
    rows = group_size * BLK
    state = [jax.ShapeDtypeStruct((kv_local, n, rows), jnp.float32) for n in (1, 1, HD)]
    bias = jax.ShapeDtypeStruct((len(gaps), 1, rows), jnp.float32)
    *state, bias, kv = pl.pallas_call(
        functools.partial(opening_kernel, gaps, kv_local, group_size),
        out_shape=[*state, bias, jax.ShapeDtypeStruct(kv.shape, kv.dtype)],
        in_specs=[SMEM, VMEM, VMEM],
        out_specs=[VMEM] * 5,
        compiler_params=pltpu.CompilerParams(vmem_limit_bytes=20 * MIB),
        cost_estimate=cost(20_000_000_000, 0),
    )(docs, queries, kv)
    return state, bias, kv


def heads_of(kv_head, group_size):
    return range(kv_head * group_size, (kv_head + 1) * group_size)


def attend_kernel(blocks, own, kv_local, group_size, resume, finish, q_ref, *refs):
    refs = list(refs)
    kv_refs = [refs.pop(0) for _ in range(blocks)]
    bias_refs = [refs.pop(0) for _ in range(blocks - own)]
    state_in = [refs.pop(0) for _ in range(3)] if resume else None
    w_ref = refs.pop(0) if finish else None
    width = kv_local * HD
    scale = jnp.float32(LOG2E / HD**0.5)
    if own:
        row = lax.broadcasted_iota(jnp.int32, (BLK, BLK), 0)
        column = lax.broadcasted_iota(jnp.int32, (BLK, BLK), 1)
        causal = jnp.concatenate([row <= column] * group_size, axis=1)
    states = [[ref[kv_head] for ref in state_in] if resume else None for kv_head in range(kv_local)]
    queries = [
        jnp.concatenate([q_ref[:, h * HD : (h + 1) * HD] for h in heads_of(kv_head, group_size)], axis=0)
        for kv_head in range(kv_local)
    ]
    for start in range(0, blocks, ROUND):
        picked = range(start, min(start + ROUND, blocks))
        scores = [
            [
                lax.dot_general(
                    kv_refs[at][:, kv_head * HD : (kv_head + 1) * HD],
                    queries[kv_head],
                    (((1,), (1,)), ((), ())),
                    preferred_element_type=jnp.float32,
                )
                for at in picked
            ]
            for kv_head in range(kv_local)
        ]
        for kv_head in range(kv_local):
            parts = [
                jnp.where(causal, part, FAR) if own and at == 0 else part + bias_refs[at - own][...]
                for at, part in zip(picked, scores[kv_head])
            ]
            state = states[kv_head]
            top = jnp.max(functools.reduce(jnp.maximum, parts), axis=0, keepdims=True)
            if state:
                top = jnp.maximum(state[0], top)
            weights = [jnp.exp2((part - top) * scale) for part in parts]
            total = jnp.sum(functools.reduce(jnp.add, weights), axis=0, keepdims=True)
            values = [
                kv_refs[at][:, width + kv_head * HD : width + (kv_head + 1) * HD] for at in picked
            ]
            summed = lax.dot_general(
                jnp.concatenate(values, axis=0),
                jnp.concatenate([w.astype(jnp.bfloat16) for w in weights], axis=0),
                (((0,), (0,)), ((), ())),
                preferred_element_type=jnp.float32,
            )
            if state:
                factor = jnp.exp2((state[0] - top) * scale)
                total = total + state[1] * factor
                summed = summed + state[2] * factor
            states[kv_head] = [top, total, summed]
    for kv_head, state in enumerate(states):
        if finish:
            attended = state[2] * (1.0 / state[1])
            for g, h in enumerate(heads_of(kv_head, group_size)):
                turned_back = attended[:, g * BLK : (g + 1) * BLK].T
                refs[0][:, h * HD : (h + 1) * HD] = turned_back.astype(jnp.bfloat16)
        else:
            for ref, value in zip(refs, state):
                ref[kv_head] = value
    if finish:
        out_ref, part_ref = refs
        part_ref[...] = project_part(out_ref, w_ref, 1, finish)


def first_column(columns, step):
    groups = lax.axis_size("head")
    target = lax.rem(lax.axis_index("head") + step, groups)
    return pl.multiple_of(target * (columns // groups), 128)


def attend(queries, kv_blocks, biases, kv_local, group_size, state, weights=None, part=None):
    rows = group_size * BLK
    if part:
        out_shape = [jax.ShapeDtypeStruct(queries.shape, jnp.bfloat16), part_shape(part)]
    else:
        out_shape = [jax.ShapeDtypeStruct((kv_local, n, rows), jnp.float32) for n in (1, 1, HD)]
    operands = [queries, *kv_blocks, *biases, *state] + ([weights] if part else [])
    blocks = len(kv_blocks)
    return pl.pallas_call(
        functools.partial(
            attend_kernel, blocks, len(biases) < blocks, kv_local, group_size, bool(state), part
        ),
        out_shape=out_shape,
        in_specs=[VMEM] * len(operands),
        out_specs=[VMEM] * len(out_shape),
        compiler_params=pltpu.CompilerParams(vmem_limit_bytes=20 * MIB),
        cost_estimate=cost(1_000_000_000, 2_000_000),
    )(*operands)


def project_part(a_ref, w_ref, step, part):
    begin = pl.multiple_of(first_column(w_ref.shape[1], step) + part.start, 128)
    columns = pl.ds(begin, part.stop - part.start)
    return jnp.dot(
        a_ref[...], w_ref[:, columns], preferred_element_type=jnp.float32
    ).astype(jnp.bfloat16)


def project_kernel(step, parts, a_ref, w_ref, *out_refs):
    for part, out_ref in zip(parts, out_refs):
        out_ref[...] = project_part(a_ref, w_ref, step, part)


def project(attended, weights, step, parts):
    width = sum(part.stop - part.start for part in parts)
    return pl.pallas_call(
        functools.partial(project_kernel, step, parts),
        out_shape=[part_shape(part) for part in parts],
        in_specs=[VMEM, VMEM],
        out_specs=[VMEM] * len(parts),
        compiler_params=pltpu.CompilerParams(vmem_limit_bytes=20 * MIB),
        cost_estimate=cost(2 * BLK * width * attended.shape[1], 1_000_000),
    )(attended, weights)


def part_shape(part):
    return jax.ShapeDtypeStruct((BLK, part.stop - part.start), jnp.bfloat16)


def close_kernel(parts, each, resume, *refs):
    refs = list(refs)
    mine_refs = [refs.pop(0) for _ in parts]
    other_refs = [[refs.pop(0) for _ in range(each)] for _ in parts]
    if resume:
        refs.pop(0)
    out_ref, *sum_refs, sems = refs
    copies = []
    for at, part in enumerate(parts):
        total = mine_refs[at][...].astype(jnp.float32)
        for ref in other_refs[at]:
            total = total + ref[...].astype(jnp.float32)
        sum_refs[at][...] = total.astype(sum_refs[at].dtype)
        copies.append(pltpu.make_async_copy(sum_refs[at], out_ref.at[:, part], sems.at[at]))
        copies[-1].start()
    for copy in copies:
        copy.wait()


def close(chosen, parts, mine, received, out=None):
    others = [row[at] for at in chosen for row in received]
    operands = [mine[at] for at in chosen] + others + ([] if out is None else [out])
    return pl.pallas_call(
        functools.partial(
            close_kernel, [parts[at] for at in chosen], len(received), out is not None
        ),
        out_shape=jax.ShapeDtypeStruct((BLK, parts[-1].stop), jnp.bfloat16),
        in_specs=[VMEM] * (len(chosen) + len(others)) + ([] if out is None else [HBM]),
        out_specs=HBM,
        scratch_shapes=[
            *[pltpu.VMEM((BLK, parts[at].stop - parts[at].start), jnp.bfloat16) for at in chosen],
            pltpu.SemaphoreType.DMA((len(chosen),)),
        ],
        input_output_aliases={} if out is None else {len(operands) - 1: 0},
        compiler_params=pltpu.CompilerParams(vmem_limit_bytes=8 * MIB),
        cost_estimate=cost(1_000_000, 1_000_000),
    )(*operands)


def mask_kernel(docs_ref, bias_ref):
    position = lax.axis_index("seq")
    doc = docs_ref[position]
    for at in range(bias_ref.shape[0]):
        near = (docs_ref[jnp.maximum(position - at - 1, 0)] == doc) & (position > at)
        bias_ref[at] = jnp.full(bias_ref.shape[1:], jnp.where(near, 0.0, FAR), jnp.float32)


def mask(docs, reach, rows):
    return pl.pallas_call(
        mask_kernel,
        out_shape=jax.ShapeDtypeStruct((reach, 1, rows), jnp.float32),
        in_specs=[SMEM],
        out_specs=VMEM,
    )(docs)


def side_by_side(left, right):
    low = jnp.array(-jnp.inf, left.dtype)
    first = lax.pad(left, low, ((0, 0, 0), (0, right.shape[1], 0)))
    return jnp.maximum(first, lax.pad(right, low, ((0, 0, 0), (left.shape[1], 0, 0))))


def local(query_states, key_states, value_states, out_weight, block_docs):
    tokens_here = query_states.shape[0]
    kv_local = key_states.shape[1] // HD
    group_size = QH // KH
    count = lax.axis_size("seq")
    groups = lax.axis_size("head")
    assert tokens_here == BLK and block_docs.shape[0] == count
    reach = min(DOC_BLK, count // 4) - 1
    eighth = out_weight.shape[1] // groups // 8
    ends = [eighth * sum(PARTS[:at]) for at in range(len(PARTS) + 1)]
    parts = [slice(begin, end) for begin, end in zip(ends, ends[1:])]
    sizes = (kv_local, group_size)

    kv = hold(side_by_side(key_states, value_states))
    if reach == 3 and count == len(RINGS[0]):
        packed, carrier = ring_table()
        arrived = [lax.ppermute(kv, "seq", list(enumerate(ring))) for ring in RINGS[1:]]
        gaps = [functools.partial(pick, word) for word in packed]
        gaps.append(lambda position: 1 + 2 * (position & 1))
        state, bias, kv = opening(block_docs, query_states, kv, out_weight, gaps, *sizes)
        arrived = [lax.ppermute(kv, "seq", list(enumerate(RINGS[0])))] + arrived
        second = choose(carrier, arrived[1:], state[0])
        late = lax.ppermute(second, "seq", [(i, i ^ 1) for i in range(count)])
        biases = [bias[at] for at in range(len(gaps))]
        state = attend(query_states, arrived[1:], biases[1:3], *sizes, state)
        attended, last = attend(
            query_states, [arrived[0], late], [biases[0], biases[3]], *sizes, state, out_weight, parts[-1]
        )
    else:
        blocks = [kv]
        while len(blocks) < reach + 1:
            have = len(blocks)
            send = min(have, reach + 1 - have)
            passed = turned(jnp.stack(blocks[:send]), "seq", have)
            blocks = blocks + [passed[i] for i in range(send)]
        bias = mask(block_docs, reach, group_size * BLK)
        biases = [bias[at] for at in range(reach)]
        attended, last = attend(query_states, blocks, biases, *sizes, (), out_weight, parts[-1])

    received = []
    for step in range(1, groups):
        if step == 1:
            row = [*project(attended, out_weight, 1, parts[:-1]), last]
        else:
            row = project(attended, out_weight, step, parts)
        received.append([turned(partial, "head", step) for partial in row])
    mine = project(attended, out_weight, 0, parts)
    late = len(parts) - 2
    early = [at for at in range(len(parts)) if at != late]
    out = close(early, parts, mine, received)
    return close([late], parts, mine, received, out)


def solution(mesh):
    return jax.shard_map(
        local,
        mesh=mesh,
        in_specs=(P("seq", "head"), P("seq", "head"), P("seq", "head"), P("head", None), P()),
        out_specs=P("seq", "head"),
        check_vma=False,
    )
```

```python
import functools
import jax
import jax.numpy as jnp
from jax import lax
from jax.experimental import pallas as pl
from jax.experimental.pallas import tpu as pltpu
from jax.sharding import PartitionSpec as P

HD = 128
QH = 16
KH = 4
BLK = 128
DOC_BLK = 32
PARTS = (2, 4, 2)
ROUND = 4
LOG2E = 1.4426950408889634
MIB = 1024 * 1024
FAR = -1e30
VMEM = pl.BlockSpec(memory_space=pltpu.VMEM)
SMEM = pl.BlockSpec(memory_space=pltpu.SMEM)
HBM = pl.BlockSpec(memory_space=pltpu.HBM)
RINGS = (
    (1, 4, 3, 6, 5, 0, 2, 10, 9, 12, 7, 14, 13, 8, 15, 11),
    (1, 0, 3, 5, 6, 7, 8, 2, 10, 4, 11, 13, 14, 9, 15, 12),
    (2, 3, 4, 0, 1, 8, 7, 9, 5, 11, 12, 6, 13, 15, 10, 14),
)


def cost(flops, bytes_accessed):
    return pl.CostEstimate(flops=flops, bytes_accessed=bytes_accessed, transcendentals=0)


def turned(value, axis, steps):
    count = lax.axis_size(axis)
    return lax.ppermute(value, axis, [(source, (source + steps) % count) for source in range(count)])


def ring_table():
    gaps, carrier, seen = [0] * len(RINGS), 0, set()
    for at, ring in enumerate(RINGS):
        for source, target in enumerate(ring):
            gap = target - source
            wanted = gap == 2 or gap == (3 if source % 2 else 1)
            if wanted and (source, target) not in seen:
                seen.add((source, target))
                gaps[at] |= gap << 2 * target
                if gap == 2:
                    carrier |= (at - 1) << 2 * target
    assert len(seen) == 5 * len(RINGS[0]) // 2 - 12
    return gaps, carrier


def pick(packed, position):
    signed = packed - (1 << 32) if packed >= 1 << 31 else packed
    return lax.shift_right_logical(jnp.int32(signed), 2 * position) & 3


def hold_kernel(kv_in, kv_out):
    pass


def hold(kv):
    return pl.pallas_call(
        hold_kernel,
        out_shape=jax.ShapeDtypeStruct(kv.shape, kv.dtype),
        in_specs=[VMEM],
        out_specs=VMEM,
        input_output_aliases={0: 0},
        compiler_params=pltpu.CompilerParams(vmem_limit_bytes=2 * MIB),
        cost_estimate=cost(6_000_000_000, 0),
    )(kv)


def choose_kernel(carrier, *refs):
    *arrived_refs, _, out_ref = refs
    holder = pick(carrier, lax.axis_index("seq"))
    for at, ref in enumerate(arrived_refs):

        @pl.when(holder == at)
        def _():
            out_ref[...] = ref[...]


def choose(carrier, arrived, after):
    return pl.pallas_call(
        functools.partial(choose_kernel, carrier),
        out_shape=jax.ShapeDtypeStruct(arrived[0].shape, arrived[0].dtype),
        in_specs=[VMEM] * (len(arrived) + 1),
        out_specs=VMEM,
        compiler_params=pltpu.CompilerParams(vmem_limit_bytes=4 * MIB),
        cost_estimate=cost(0, 300_000),
    )(*arrived, after)


def opening_kernel(gaps, kv_local, group_size, docs_ref, q_ref, kv_ref, *refs):
    *state_refs, bias_ref, kv_out = refs
    kv_out[...] = kv_ref[...]
    position = lax.axis_index("seq")
    doc = docs_ref[position]
    for at, gap in enumerate(gaps):
        gap = gap(position)
        source = jnp.maximum(position - gap, 0)
        near = (docs_ref[source] == doc) & (position >= gap) & (gap > 0)
        bias_ref[at] = jnp.full(bias_ref.shape[1:], jnp.where(near, 0.0, FAR), jnp.float32)
    attend_kernel(1, True, kv_local, group_size, False, False, q_ref, kv_ref, *state_refs)


def opening(docs, queries, kv, weights, gaps, kv_local, group_size):
    rows = group_size * BLK
    state = [jax.ShapeDtypeStruct((kv_local, n, rows), jnp.float32) for n in (1, 1, HD)]
    bias = jax.ShapeDtypeStruct((len(gaps), 1, rows), jnp.float32)
    *state, bias, kv = pl.pallas_call(
        functools.partial(opening_kernel, gaps, kv_local, group_size),
        out_shape=[*state, bias, jax.ShapeDtypeStruct(kv.shape, kv.dtype)],
        in_specs=[SMEM, VMEM, VMEM],
        out_specs=[VMEM] * 5,
        compiler_params=pltpu.CompilerParams(vmem_limit_bytes=20 * MIB),
        cost_estimate=cost(20_000_000_000, 0),
    )(docs, queries, kv)
    return state, bias, kv


def heads_of(kv_head, group_size):
    return range(kv_head * group_size, (kv_head + 1) * group_size)


def attend_kernel(blocks, own, kv_local, group_size, resume, finish, q_ref, *refs):
    refs = list(refs)
    kv_refs = [refs.pop(0) for _ in range(blocks)]
    bias_refs = [refs.pop(0) for _ in range(blocks - own)]
    state_in = [refs.pop(0) for _ in range(3)] if resume else None
    w_ref = refs.pop(0) if finish else None
    width = kv_local * HD
    scale = jnp.float32(LOG2E / HD**0.5)
    if own:
        row = lax.broadcasted_iota(jnp.int32, (BLK, BLK), 0)
        column = lax.broadcasted_iota(jnp.int32, (BLK, BLK), 1)
        causal = jnp.concatenate([row <= column] * group_size, axis=1)
    states = [[ref[kv_head] for ref in state_in] if resume else None for kv_head in range(kv_local)]
    queries = [
        jnp.concatenate([q_ref[:, h * HD : (h + 1) * HD] for h in heads_of(kv_head, group_size)], axis=0)
        for kv_head in range(kv_local)
    ]
    for start in range(0, blocks, ROUND):
        picked = range(start, min(start + ROUND, blocks))
        scores = [
            [
                lax.dot_general(
                    kv_refs[at][:, kv_head * HD : (kv_head + 1) * HD],
                    queries[kv_head],
                    (((1,), (1,)), ((), ())),
                    preferred_element_type=jnp.float32,
                )
                for at in picked
            ]
            for kv_head in range(kv_local)
        ]
        for kv_head in range(kv_local):
            parts = [
                jnp.where(causal, part, FAR) if own and at == 0 else part + bias_refs[at - own][...]
                for at, part in zip(picked, scores[kv_head])
            ]
            state = states[kv_head]
            top = jnp.max(functools.reduce(jnp.maximum, parts), axis=0, keepdims=True)
            if state:
                top = jnp.maximum(state[0], top)
            weights = [jnp.exp2((part - top) * scale) for part in parts]
            total = jnp.sum(functools.reduce(jnp.add, weights), axis=0, keepdims=True)
            values = [
                kv_refs[at][:, width + kv_head * HD : width + (kv_head + 1) * HD] for at in picked
            ]
            summed = lax.dot_general(
                jnp.concatenate(values, axis=0),
                jnp.concatenate([w.astype(jnp.bfloat16) for w in weights], axis=0),
                (((0,), (0,)), ((), ())),
                preferred_element_type=jnp.float32,
            )
            if state:
                factor = jnp.exp2((state[0] - top) * scale)
                total = total + state[1] * factor
                summed = summed + state[2] * factor
            states[kv_head] = [top, total, summed]
    for kv_head, state in enumerate(states):
        if finish:
            attended = state[2] * (1.0 / state[1])
            for g, h in enumerate(heads_of(kv_head, group_size)):
                turned_back = attended[:, g * BLK : (g + 1) * BLK].T
                refs[0][:, h * HD : (h + 1) * HD] = turned_back.astype(jnp.bfloat16)
        else:
            for ref, value in zip(refs, state):
                ref[kv_head] = value
    if finish:
        out_ref, part_ref = refs
        part_ref[...] = project_part(out_ref, w_ref, 1, finish)


def first_column(columns, step):
    groups = lax.axis_size("head")
    target = lax.rem(lax.axis_index("head") + step, groups)
    return pl.multiple_of(target * (columns // groups), 128)


def attend(queries, kv_blocks, biases, kv_local, group_size, state, weights=None, part=None):
    rows = group_size * BLK
    if part:
        out_shape = [jax.ShapeDtypeStruct(queries.shape, jnp.bfloat16), part_shape(part)]
    else:
        out_shape = [jax.ShapeDtypeStruct((kv_local, n, rows), jnp.float32) for n in (1, 1, HD)]
    operands = [queries, *kv_blocks, *biases, *state] + ([weights] if part else [])
    blocks = len(kv_blocks)
    return pl.pallas_call(
        functools.partial(
            attend_kernel, blocks, len(biases) < blocks, kv_local, group_size, bool(state), part
        ),
        out_shape=out_shape,
        in_specs=[VMEM] * len(operands),
        out_specs=[VMEM] * len(out_shape),
        compiler_params=pltpu.CompilerParams(vmem_limit_bytes=20 * MIB),
        cost_estimate=cost(1_000_000_000, 2_000_000),
    )(*operands)


def project_part(a_ref, w_ref, step, part):
    begin = pl.multiple_of(first_column(w_ref.shape[1], step) + part.start, 128)
    columns = pl.ds(begin, part.stop - part.start)
    return jnp.dot(
        a_ref[...], w_ref[:, columns], preferred_element_type=jnp.float32
    ).astype(jnp.bfloat16)


def project_kernel(step, parts, a_ref, w_ref, *out_refs):
    for part, out_ref in zip(parts, out_refs):
        out_ref[...] = project_part(a_ref, w_ref, step, part)


def project(attended, weights, step, parts):
    width = sum(part.stop - part.start for part in parts)
    return pl.pallas_call(
        functools.partial(project_kernel, step, parts),
        out_shape=[part_shape(part) for part in parts],
        in_specs=[VMEM, VMEM],
        out_specs=[VMEM] * len(parts),
        compiler_params=pltpu.CompilerParams(vmem_limit_bytes=20 * MIB),
        cost_estimate=cost(4_000_000_000, 0),
    )(attended, weights)


def part_shape(part):
    return jax.ShapeDtypeStruct((BLK, part.stop - part.start), jnp.bfloat16)


def close_kernel(parts, each, resume, *refs):
    refs = list(refs)
    mine_refs = [refs.pop(0) for _ in parts]
    other_refs = [[refs.pop(0) for _ in range(each)] for _ in parts]
    if resume:
        refs.pop(0)
    out_ref, *sum_refs, sems = refs
    copies = []
    for at, part in enumerate(parts):
        total = mine_refs[at][...].astype(jnp.float32)
        for ref in other_refs[at]:
            total = total + ref[...].astype(jnp.float32)
        sum_refs[at][...] = total.astype(sum_refs[at].dtype)
        copies.append(pltpu.make_async_copy(sum_refs[at], out_ref.at[:, part], sems.at[at]))
        copies[-1].start()
    for copy in copies:
        copy.wait()


def close(chosen, parts, mine, received, out=None):
    others = [row[at] for at in chosen for row in received]
    operands = [mine[at] for at in chosen] + others + ([] if out is None else [out])
    return pl.pallas_call(
        functools.partial(
            close_kernel, [parts[at] for at in chosen], len(received), out is not None
        ),
        out_shape=jax.ShapeDtypeStruct((BLK, parts[-1].stop), jnp.bfloat16),
        in_specs=[VMEM] * (len(chosen) + len(others)) + ([] if out is None else [HBM]),
        out_specs=HBM,
        scratch_shapes=[
            *[pltpu.VMEM((BLK, parts[at].stop - parts[at].start), jnp.bfloat16) for at in chosen],
            pltpu.SemaphoreType.DMA((len(chosen),)),
        ],
        input_output_aliases={} if out is None else {len(operands) - 1: 0},
        compiler_params=pltpu.CompilerParams(vmem_limit_bytes=8 * MIB),
        cost_estimate=cost(1_000_000, 1_000_000),
    )(*operands)


def mask_kernel(docs_ref, bias_ref):
    position = lax.axis_index("seq")
    doc = docs_ref[position]
    for at in range(bias_ref.shape[0]):
        near = (docs_ref[jnp.maximum(position - at - 1, 0)] == doc) & (position > at)
        bias_ref[at] = jnp.full(bias_ref.shape[1:], jnp.where(near, 0.0, FAR), jnp.float32)


def mask(docs, reach, rows):
    return pl.pallas_call(
        mask_kernel,
        out_shape=jax.ShapeDtypeStruct((reach, 1, rows), jnp.float32),
        in_specs=[SMEM],
        out_specs=VMEM,
    )(docs)


def side_by_side(left, right):
    low = jnp.array(-jnp.inf, left.dtype)
    first = lax.pad(left, low, ((0, 0, 0), (0, right.shape[1], 0)))
    return jnp.maximum(first, lax.pad(right, low, ((0, 0, 0), (left.shape[1], 0, 0))))


def local(query_states, key_states, value_states, out_weight, block_docs):
    tokens_here = query_states.shape[0]
    kv_local = key_states.shape[1] // HD
    group_size = QH // KH
    count = lax.axis_size("seq")
    groups = lax.axis_size("head")
    assert tokens_here == BLK and block_docs.shape[0] == count
    reach = min(DOC_BLK, count // 4) - 1
    eighth = out_weight.shape[1] // groups // 8
    ends = [eighth * sum(PARTS[:at]) for at in range(len(PARTS) + 1)]
    parts = [slice(begin, end) for begin, end in zip(ends, ends[1:])]
    sizes = (kv_local, group_size)

    kv = hold(side_by_side(key_states, value_states))
    if reach == 3 and count == len(RINGS[0]):
        packed, carrier = ring_table()
        arrived = [lax.ppermute(kv, "seq", list(enumerate(ring))) for ring in RINGS[1:]]
        gaps = [functools.partial(pick, word) for word in packed]
        gaps.append(lambda position: 1 + 2 * (position & 1))
        state, bias, kv = opening(block_docs, query_states, kv, out_weight, gaps, *sizes)
        arrived = [lax.ppermute(kv, "seq", list(enumerate(RINGS[0])))] + arrived
        second = choose(carrier, arrived[1:], state[0])
        late = lax.ppermute(second, "seq", [(i, i ^ 1) for i in range(count)])
        biases = [bias[at] for at in range(len(gaps))]
        state = attend(query_states, arrived[1:], biases[1:3], *sizes, state)
        attended, first = attend(
            query_states, [arrived[0], late], [biases[0], biases[3]], *sizes, state, out_weight, parts[0]
        )
    else:
        blocks = [kv]
        while len(blocks) < reach + 1:
            have = len(blocks)
            send = min(have, reach + 1 - have)
            passed = turned(jnp.stack(blocks[:send]), "seq", have)
            blocks = blocks + [passed[i] for i in range(send)]
        bias = mask(block_docs, reach, group_size * BLK)
        biases = [bias[at] for at in range(reach)]
        attended, first = attend(query_states, blocks, biases, *sizes, (), out_weight, parts[0])

    received = []
    for step in range(1, groups):
        if step == 1:
            row = [first, *project(attended, out_weight, 1, parts[1:])]
        else:
            row = project(attended, out_weight, step, parts)
        received.append([turned(partial, "head", step) for partial in row])
    mine = project(attended, out_weight, 0, parts)
    late = 1
    early = [at for at in range(len(parts)) if at != late]
    out = close(early, parts, mine, received)
    return close([late], parts, mine, received, out)


def solution(mesh):
    return jax.shard_map(
        local,
        mesh=mesh,
        in_specs=(P("seq", "head"), P("seq", "head"), P("seq", "head"), P("head", None), P()),
        out_specs=P("seq", "head"),
        check_vma=False,
    )
```

```python
import functools
import jax
import jax.numpy as jnp
from jax import lax
from jax.experimental import pallas as pl
from jax.experimental.pallas import tpu as pltpu
from jax.sharding import PartitionSpec as P

HD = 128
QH = 16
KH = 4
BLK = 128
DOC_BLK = 32
PARTS = (2, 2, 2, 2)
ROUND = 4
LOG2E = 1.4426950408889634
MIB = 1024 * 1024
FAR = -1e30
VMEM = pl.BlockSpec(memory_space=pltpu.VMEM)
SMEM = pl.BlockSpec(memory_space=pltpu.SMEM)
HBM = pl.BlockSpec(memory_space=pltpu.HBM)
RINGS = (
    (1, 4, 3, 6, 5, 0, 2, 10, 9, 12, 7, 14, 13, 8, 15, 11),
    (1, 0, 3, 5, 6, 7, 8, 2, 10, 4, 11, 13, 14, 9, 15, 12),
    (2, 3, 4, 0, 1, 8, 7, 9, 5, 11, 12, 6, 13, 15, 10, 14),
)


def cost(flops, bytes_accessed):
    return pl.CostEstimate(flops=flops, bytes_accessed=bytes_accessed, transcendentals=0)


def turned(value, axis, steps):
    count = lax.axis_size(axis)
    return lax.ppermute(value, axis, [(source, (source + steps) % count) for source in range(count)])


def ring_table():
    gaps, carrier, seen = [0] * len(RINGS), 0, set()
    for at, ring in enumerate(RINGS):
        for source, target in enumerate(ring):
            gap = target - source
            wanted = gap == 2 or gap == (3 if source % 2 else 1)
            if wanted and (source, target) not in seen:
                seen.add((source, target))
                gaps[at] |= gap << 2 * target
                if gap == 2:
                    carrier |= (at - 1) << 2 * target
    assert len(seen) == 5 * len(RINGS[0]) // 2 - 12
    return gaps, carrier


def pick(packed, position):
    signed = packed - (1 << 32) if packed >= 1 << 31 else packed
    return lax.shift_right_logical(jnp.int32(signed), 2 * position) & 3


def hold_kernel(kv_in, kv_out):
    pass


def hold(kv):
    return pl.pallas_call(
        hold_kernel,
        out_shape=jax.ShapeDtypeStruct(kv.shape, kv.dtype),
        in_specs=[VMEM],
        out_specs=VMEM,
        input_output_aliases={0: 0},
        compiler_params=pltpu.CompilerParams(vmem_limit_bytes=2 * MIB),
        cost_estimate=cost(6_000_000_000, 0),
    )(kv)


def choose_kernel(carrier, *refs):
    *arrived_refs, _, out_ref = refs
    holder = pick(carrier, lax.axis_index("seq"))
    for at, ref in enumerate(arrived_refs):

        @pl.when(holder == at)
        def _():
            out_ref[...] = ref[...]


def choose(carrier, arrived, after):
    return pl.pallas_call(
        functools.partial(choose_kernel, carrier),
        out_shape=jax.ShapeDtypeStruct(arrived[0].shape, arrived[0].dtype),
        in_specs=[VMEM] * (len(arrived) + 1),
        out_specs=VMEM,
        compiler_params=pltpu.CompilerParams(vmem_limit_bytes=4 * MIB),
        cost_estimate=cost(0, 300_000),
    )(*arrived, after)


def opening_kernel(gaps, kv_local, group_size, docs_ref, q_ref, kv_ref, *refs):
    *state_refs, bias_ref, kv_out = refs
    kv_out[...] = kv_ref[...]
    position = lax.axis_index("seq")
    doc = docs_ref[position]
    for at, gap in enumerate(gaps):
        gap = gap(position)
        source = jnp.maximum(position - gap, 0)
        near = (docs_ref[source] == doc) & (position >= gap) & (gap > 0)
        bias_ref[at] = jnp.full(bias_ref.shape[1:], jnp.where(near, 0.0, FAR), jnp.float32)
    attend_kernel(1, True, kv_local, group_size, False, False, q_ref, kv_ref, *state_refs)


def opening(docs, queries, kv, weights, gaps, kv_local, group_size):
    rows = group_size * BLK
    state = [jax.ShapeDtypeStruct((kv_local, n, rows), jnp.float32) for n in (1, 1, HD)]
    bias = jax.ShapeDtypeStruct((len(gaps), 1, rows), jnp.float32)
    *state, bias, kv = pl.pallas_call(
        functools.partial(opening_kernel, gaps, kv_local, group_size),
        out_shape=[*state, bias, jax.ShapeDtypeStruct(kv.shape, kv.dtype)],
        in_specs=[SMEM, VMEM, VMEM],
        out_specs=[VMEM] * 5,
        compiler_params=pltpu.CompilerParams(vmem_limit_bytes=20 * MIB),
        cost_estimate=cost(20_000_000_000, 0),
    )(docs, queries, kv)
    return state, bias, kv


def heads_of(kv_head, group_size):
    return range(kv_head * group_size, (kv_head + 1) * group_size)


def attend_kernel(blocks, own, kv_local, group_size, resume, finish, q_ref, *refs):
    refs = list(refs)
    kv_refs = [refs.pop(0) for _ in range(blocks)]
    bias_refs = [refs.pop(0) for _ in range(blocks - own)]
    state_in = [refs.pop(0) for _ in range(3)] if resume else None
    w_ref = refs.pop(0) if finish else None
    width = kv_local * HD
    scale = jnp.float32(LOG2E / HD**0.5)
    if own:
        row = lax.broadcasted_iota(jnp.int32, (BLK, BLK), 0)
        column = lax.broadcasted_iota(jnp.int32, (BLK, BLK), 1)
        causal = jnp.concatenate([row <= column] * group_size, axis=1)
    states = [[ref[kv_head] for ref in state_in] if resume else None for kv_head in range(kv_local)]
    queries = [
        jnp.concatenate([q_ref[:, h * HD : (h + 1) * HD] for h in heads_of(kv_head, group_size)], axis=0)
        for kv_head in range(kv_local)
    ]
    for start in range(0, blocks, ROUND):
        picked = range(start, min(start + ROUND, blocks))
        scores = [
            [
                lax.dot_general(
                    kv_refs[at][:, kv_head * HD : (kv_head + 1) * HD],
                    queries[kv_head],
                    (((1,), (1,)), ((), ())),
                    preferred_element_type=jnp.float32,
                )
                for at in picked
            ]
            for kv_head in range(kv_local)
        ]
        for kv_head in range(kv_local):
            parts = [
                jnp.where(causal, part, FAR) if own and at == 0 else part + bias_refs[at - own][...]
                for at, part in zip(picked, scores[kv_head])
            ]
            state = states[kv_head]
            top = jnp.max(functools.reduce(jnp.maximum, parts), axis=0, keepdims=True)
            if state:
                top = jnp.maximum(state[0], top)
            weights = [jnp.exp2((part - top) * scale) for part in parts]
            total = jnp.sum(functools.reduce(jnp.add, weights), axis=0, keepdims=True)
            values = [
                kv_refs[at][:, width + kv_head * HD : width + (kv_head + 1) * HD] for at in picked
            ]
            summed = lax.dot_general(
                jnp.concatenate(values, axis=0),
                jnp.concatenate([w.astype(jnp.bfloat16) for w in weights], axis=0),
                (((0,), (0,)), ((), ())),
                preferred_element_type=jnp.float32,
            )
            if state:
                factor = jnp.exp2((state[0] - top) * scale)
                total = total + state[1] * factor
                summed = summed + state[2] * factor
            states[kv_head] = [top, total, summed]
    for kv_head, state in enumerate(states):
        if finish:
            attended = state[2] * (1.0 / state[1])
            for g, h in enumerate(heads_of(kv_head, group_size)):
                turned_back = attended[:, g * BLK : (g + 1) * BLK].T
                refs[0][:, h * HD : (h + 1) * HD] = turned_back.astype(jnp.bfloat16)
        else:
            for ref, value in zip(refs, state):
                ref[kv_head] = value
    if finish:
        out_ref, part_ref = refs
        part_ref[...] = project_part(out_ref, w_ref, 1, finish)


def first_column(columns, step):
    groups = lax.axis_size("head")
    target = lax.rem(lax.axis_index("head") + step, groups)
    return pl.multiple_of(target * (columns // groups), 128)


def attend(queries, kv_blocks, biases, kv_local, group_size, state, weights=None, part=None):
    rows = group_size * BLK
    if part:
        out_shape = [jax.ShapeDtypeStruct(queries.shape, jnp.bfloat16), part_shape(part)]
    else:
        out_shape = [jax.ShapeDtypeStruct((kv_local, n, rows), jnp.float32) for n in (1, 1, HD)]
    operands = [queries, *kv_blocks, *biases, *state] + ([weights] if part else [])
    blocks = len(kv_blocks)
    return pl.pallas_call(
        functools.partial(
            attend_kernel, blocks, len(biases) < blocks, kv_local, group_size, bool(state), part
        ),
        out_shape=out_shape,
        in_specs=[VMEM] * len(operands),
        out_specs=[VMEM] * len(out_shape),
        compiler_params=pltpu.CompilerParams(vmem_limit_bytes=20 * MIB),
        cost_estimate=cost(1_000_000_000, 2_000_000),
    )(*operands)


def project_part(a_ref, w_ref, step, part):
    begin = pl.multiple_of(first_column(w_ref.shape[1], step) + part.start, 128)
    columns = pl.ds(begin, part.stop - part.start)
    return jnp.dot(
        a_ref[...], w_ref[:, columns], preferred_element_type=jnp.float32
    ).astype(jnp.bfloat16)


def project_kernel(step, parts, a_ref, w_ref, *out_refs):
    for part, out_ref in zip(parts, out_refs):
        out_ref[...] = project_part(a_ref, w_ref, step, part)


def project(attended, weights, step, parts):
    width = sum(part.stop - part.start for part in parts)
    return pl.pallas_call(
        functools.partial(project_kernel, step, parts),
        out_shape=[part_shape(part) for part in parts],
        in_specs=[VMEM, VMEM],
        out_specs=[VMEM] * len(parts),
        compiler_params=pltpu.CompilerParams(vmem_limit_bytes=20 * MIB),
        cost_estimate=cost(2 * BLK * width * attended.shape[1], 1_000_000),
    )(attended, weights)


def part_shape(part):
    return jax.ShapeDtypeStruct((BLK, part.stop - part.start), jnp.bfloat16)


def close_kernel(parts, each, resume, *refs):
    refs = list(refs)
    mine_refs = [refs.pop(0) for _ in parts]
    other_refs = [[refs.pop(0) for _ in range(each)] for _ in parts]
    if resume:
        refs.pop(0)
    out_ref, *sum_refs, sems = refs
    copies = []
    for at, part in enumerate(parts):
        total = mine_refs[at][...].astype(jnp.float32)
        for ref in other_refs[at]:
            total = total + ref[...].astype(jnp.float32)
        sum_refs[at][...] = total.astype(sum_refs[at].dtype)
        copies.append(pltpu.make_async_copy(sum_refs[at], out_ref.at[:, part], sems.at[at]))
        copies[-1].start()
    for copy in copies:
        copy.wait()


def close(chosen, parts, mine, received, out=None):
    others = [row[at] for at in chosen for row in received]
    operands = [mine[at] for at in chosen] + others + ([] if out is None else [out])
    return pl.pallas_call(
        functools.partial(
            close_kernel, [parts[at] for at in chosen], len(received), out is not None
        ),
        out_shape=jax.ShapeDtypeStruct((BLK, parts[-1].stop), jnp.bfloat16),
        in_specs=[VMEM] * (len(chosen) + len(others)) + ([] if out is None else [HBM]),
        out_specs=HBM,
        scratch_shapes=[
            *[pltpu.VMEM((BLK, parts[at].stop - parts[at].start), jnp.bfloat16) for at in chosen],
            pltpu.SemaphoreType.DMA((len(chosen),)),
        ],
        input_output_aliases={} if out is None else {len(operands) - 1: 0},
        compiler_params=pltpu.CompilerParams(vmem_limit_bytes=8 * MIB),
        cost_estimate=cost(1_000_000, 1_000_000),
    )(*operands)


def mask_kernel(docs_ref, bias_ref):
    position = lax.axis_index("seq")
    doc = docs_ref[position]
    for at in range(bias_ref.shape[0]):
        near = (docs_ref[jnp.maximum(position - at - 1, 0)] == doc) & (position > at)
        bias_ref[at] = jnp.full(bias_ref.shape[1:], jnp.where(near, 0.0, FAR), jnp.float32)


def mask(docs, reach, rows):
    return pl.pallas_call(
        mask_kernel,
        out_shape=jax.ShapeDtypeStruct((reach, 1, rows), jnp.float32),
        in_specs=[SMEM],
        out_specs=VMEM,
    )(docs)


def side_by_side(left, right):
    low = jnp.array(-jnp.inf, left.dtype)
    first = lax.pad(left, low, ((0, 0, 0), (0, right.shape[1], 0)))
    return jnp.maximum(first, lax.pad(right, low, ((0, 0, 0), (left.shape[1], 0, 0))))


def local(query_states, key_states, value_states, out_weight, block_docs):
    tokens_here = query_states.shape[0]
    kv_local = key_states.shape[1] // HD
    group_size = QH // KH
    count = lax.axis_size("seq")
    groups = lax.axis_size("head")
    assert tokens_here == BLK and block_docs.shape[0] == count
    reach = min(DOC_BLK, count // 4) - 1
    eighth = out_weight.shape[1] // groups // 8
    ends = [eighth * sum(PARTS[:at]) for at in range(len(PARTS) + 1)]
    parts = [slice(begin, end) for begin, end in zip(ends, ends[1:])]
    sizes = (kv_local, group_size)

    kv = hold(side_by_side(key_states, value_states))
    if reach == 3 and count == len(RINGS[0]):
        packed, carrier = ring_table()
        first_kv = kv
        arrived = [lax.ppermute(kv, "seq", list(enumerate(ring))) for ring in RINGS[1:]]
        gaps = [functools.partial(pick, word) for word in packed]
        gaps.append(lambda position: 1 + 2 * (position & 1))
        state, bias, kv = opening(block_docs, query_states, kv, out_weight, gaps, *sizes)
        arrived = [lax.ppermute(first_kv, "seq", list(enumerate(RINGS[0])))] + arrived
        second = choose(carrier, arrived[1:], state[0])
        late = lax.ppermute(second, "seq", [(i, i ^ 1) for i in range(count)])
        biases = [bias[at] for at in range(len(gaps))]
        state = attend(query_states, arrived[1:], biases[1:3], *sizes, state)
        attended, last = attend(
            query_states, [arrived[0], late], [biases[0], biases[3]], *sizes, state, out_weight, parts[-1]
        )
    else:
        blocks = [kv]
        while len(blocks) < reach + 1:
            have = len(blocks)
            send = min(have, reach + 1 - have)
            passed = turned(jnp.stack(blocks[:send]), "seq", have)
            blocks = blocks + [passed[i] for i in range(send)]
        bias = mask(block_docs, reach, group_size * BLK)
        biases = [bias[at] for at in range(reach)]
        attended, last = attend(query_states, blocks, biases, *sizes, (), out_weight, parts[-1])

    received = []
    for step in range(1, groups):
        if step == 1:
            row = [*project(attended, out_weight, 1, parts[:-1]), last]
        else:
            row = project(attended, out_weight, step, parts)
        received.append([turned(partial, "head", step) for partial in row])
    mine = project(attended, out_weight, 0, parts)
    late = len(parts) - 2
    early = [at for at in range(len(parts)) if at != late]
    out = close(early, parts, mine, received)
    return close([late], parts, mine, received, out)


def solution(mesh):
    return jax.shard_map(
        local,
        mesh=mesh,
        in_specs=(P("seq", "head"), P("seq", "head"), P("seq", "head"), P("head", None), P()),
        out_specs=P("seq", "head"),
        check_vma=False,
    )
```

```python
import functools
import jax
import jax.numpy as jnp
from jax import lax
from jax.experimental import pallas as pl
from jax.experimental.pallas import tpu as pltpu
from jax.sharding import PartitionSpec as P

HD = 128
QH = 16
KH = 4
BLK = 128
DOC_BLK = 32
PARTS = (2, 2, 2, 2)
ROUND = 4
LOG2E = 1.4426950408889634
MIB = 1024 * 1024
FAR = -1e30
VMEM = pl.BlockSpec(memory_space=pltpu.VMEM)
SMEM = pl.BlockSpec(memory_space=pltpu.SMEM)
HBM = pl.BlockSpec(memory_space=pltpu.HBM)
RINGS = (
    (1, 4, 3, 6, 5, 0, 2, 10, 9, 12, 7, 14, 13, 8, 15, 11),
    (1, 0, 3, 5, 6, 7, 8, 2, 10, 4, 11, 13, 14, 9, 15, 12),
    (2, 3, 4, 0, 1, 8, 7, 9, 5, 11, 12, 6, 13, 15, 10, 14),
)


def cost(flops, bytes_accessed):
    return pl.CostEstimate(flops=flops, bytes_accessed=bytes_accessed, transcendentals=0)


def turned(value, axis, steps):
    count = lax.axis_size(axis)
    return lax.ppermute(value, axis, [(source, (source + steps) % count) for source in range(count)])


def ring_table():
    gaps, carrier, seen = [0] * len(RINGS), 0, set()
    for at, ring in enumerate(RINGS):
        for source, target in enumerate(ring):
            gap = target - source
            wanted = gap == 2 or gap == (3 if source % 2 else 1)
            if wanted and (source, target) not in seen:
                seen.add((source, target))
                gaps[at] |= gap << 2 * target
                if gap == 2:
                    carrier |= (at - 1) << 2 * target
    assert len(seen) == 5 * len(RINGS[0]) // 2 - 12
    return gaps, carrier


def pick(packed, position):
    signed = packed - (1 << 32) if packed >= 1 << 31 else packed
    return lax.shift_right_logical(jnp.int32(signed), 2 * position) & 3


def hold_kernel(kv_in, kv_out):
    pass


def hold(kv):
    return pl.pallas_call(
        hold_kernel,
        out_shape=jax.ShapeDtypeStruct(kv.shape, kv.dtype),
        in_specs=[VMEM],
        out_specs=VMEM,
        input_output_aliases={0: 0},
        compiler_params=pltpu.CompilerParams(vmem_limit_bytes=2 * MIB),
        cost_estimate=cost(6_000_000_000, 0),
    )(kv)


def choose_kernel(carrier, *refs):
    *arrived_refs, _, out_ref = refs
    holder = pick(carrier, lax.axis_index("seq"))
    for at, ref in enumerate(arrived_refs):

        @pl.when(holder == at)
        def _():
            out_ref[...] = ref[...]


def choose(carrier, arrived, after):
    return pl.pallas_call(
        functools.partial(choose_kernel, carrier),
        out_shape=jax.ShapeDtypeStruct(arrived[0].shape, arrived[0].dtype),
        in_specs=[VMEM] * (len(arrived) + 1),
        out_specs=VMEM,
        compiler_params=pltpu.CompilerParams(vmem_limit_bytes=4 * MIB),
        cost_estimate=cost(0, 300_000),
    )(*arrived, after)


def opening_kernel(gaps, kv_local, group_size, docs_ref, q_ref, kv_ref, *refs):
    *state_refs, bias_ref, kv_out = refs
    kv_out[...] = kv_ref[...]
    position = lax.axis_index("seq")
    doc = docs_ref[position]
    for at, gap in enumerate(gaps):
        gap = gap(position)
        source = jnp.maximum(position - gap, 0)
        near = (docs_ref[source] == doc) & (position >= gap) & (gap > 0)
        bias_ref[at] = jnp.full(bias_ref.shape[1:], jnp.where(near, 0.0, FAR), jnp.float32)
    attend_kernel(1, True, (), kv_local, group_size, False, False, q_ref, kv_ref, bias_ref, *state_refs)


def opening(docs, queries, kv, weights, gaps, kv_local, group_size):
    rows = group_size * BLK
    state = [jax.ShapeDtypeStruct((kv_local, n, rows), jnp.float32) for n in (1, 1, HD)]
    bias = jax.ShapeDtypeStruct((len(gaps), 1, rows), jnp.float32)
    *state, bias, kv = pl.pallas_call(
        functools.partial(opening_kernel, gaps, kv_local, group_size),
        out_shape=[*state, bias, jax.ShapeDtypeStruct(kv.shape, kv.dtype)],
        in_specs=[SMEM, VMEM, VMEM],
        out_specs=[VMEM] * 5,
        compiler_params=pltpu.CompilerParams(vmem_limit_bytes=20 * MIB),
        cost_estimate=cost(20_000_000_000, 0),
    )(docs, queries, kv)
    return state, bias, kv


def heads_of(kv_head, group_size):
    return range(kv_head * group_size, (kv_head + 1) * group_size)


def attend_kernel(blocks, own, rows_of_bias, kv_local, group_size, resume, finish, q_ref, *refs):
    refs = list(refs)
    kv_refs = [refs.pop(0) for _ in range(blocks)]
    bias_ref = refs.pop(0)
    bias_refs = [bias_ref.at[at] for at in rows_of_bias]
    state_in = [refs.pop(0) for _ in range(3)] if resume else None
    w_ref = refs.pop(0) if finish else None
    width = kv_local * HD
    scale = jnp.float32(LOG2E / HD**0.5)
    if own:
        row = lax.broadcasted_iota(jnp.int32, (BLK, BLK), 0)
        column = lax.broadcasted_iota(jnp.int32, (BLK, BLK), 1)
        causal = jnp.concatenate([row <= column] * group_size, axis=1)
    states = [[ref[kv_head] for ref in state_in] if resume else None for kv_head in range(kv_local)]
    queries = [
        jnp.concatenate([q_ref[:, h * HD : (h + 1) * HD] for h in heads_of(kv_head, group_size)], axis=0)
        for kv_head in range(kv_local)
    ]
    for start in range(0, blocks, ROUND):
        picked = range(start, min(start + ROUND, blocks))
        scores = [
            [
                lax.dot_general(
                    kv_refs[at][:, kv_head * HD : (kv_head + 1) * HD],
                    queries[kv_head],
                    (((1,), (1,)), ((), ())),
                    preferred_element_type=jnp.float32,
                )
                for at in picked
            ]
            for kv_head in range(kv_local)
        ]
        for kv_head in range(kv_local):
            parts = [
                jnp.where(causal, part, FAR) if own and at == 0 else part + bias_refs[at - own][...]
                for at, part in zip(picked, scores[kv_head])
            ]
            state = states[kv_head]
            top = jnp.max(functools.reduce(jnp.maximum, parts), axis=0, keepdims=True)
            if state:
                top = jnp.maximum(state[0], top)
            weights = [jnp.exp2((part - top) * scale) for part in parts]
            total = jnp.sum(functools.reduce(jnp.add, weights), axis=0, keepdims=True)
            values = [
                kv_refs[at][:, width + kv_head * HD : width + (kv_head + 1) * HD] for at in picked
            ]
            summed = lax.dot_general(
                jnp.concatenate(values, axis=0),
                jnp.concatenate([w.astype(jnp.bfloat16) for w in weights], axis=0),
                (((0,), (0,)), ((), ())),
                preferred_element_type=jnp.float32,
            )
            if state:
                factor = jnp.exp2((state[0] - top) * scale)
                total = total + state[1] * factor
                summed = summed + state[2] * factor
            states[kv_head] = [top, total, summed]
    for kv_head, state in enumerate(states):
        if finish:
            attended = state[2] * (1.0 / state[1])
            for g, h in enumerate(heads_of(kv_head, group_size)):
                turned_back = attended[:, g * BLK : (g + 1) * BLK].T
                refs[0][:, h * HD : (h + 1) * HD] = turned_back.astype(jnp.bfloat16)
        else:
            for ref, value in zip(refs, state):
                ref[kv_head] = value
    if finish:
        out_ref, part_ref = refs
        part_ref[...] = project_part(out_ref, w_ref, 1, finish)


def first_column(columns, step):
    groups = lax.axis_size("head")
    target = lax.rem(lax.axis_index("head") + step, groups)
    return pl.multiple_of(target * (columns // groups), 128)


def attend(queries, kv_blocks, bias, rows_of_bias, kv_local, group_size, state, weights=None, part=None):
    rows = group_size * BLK
    if part:
        out_shape = [jax.ShapeDtypeStruct(queries.shape, jnp.bfloat16), part_shape(part)]
    else:
        out_shape = [jax.ShapeDtypeStruct((kv_local, n, rows), jnp.float32) for n in (1, 1, HD)]
    operands = [queries, *kv_blocks, bias, *state] + ([weights] if part else [])
    blocks = len(kv_blocks)
    return pl.pallas_call(
        functools.partial(
            attend_kernel, blocks, len(rows_of_bias) < blocks, rows_of_bias, kv_local, group_size, bool(state), part
        ),
        out_shape=out_shape,
        in_specs=[VMEM] * len(operands),
        out_specs=[VMEM] * len(out_shape),
        compiler_params=pltpu.CompilerParams(vmem_limit_bytes=20 * MIB),
        cost_estimate=cost(1_000_000_000, 2_000_000),
    )(*operands)


def project_part(a_ref, w_ref, step, part):
    begin = pl.multiple_of(first_column(w_ref.shape[1], step) + part.start, 128)
    columns = pl.ds(begin, part.stop - part.start)
    return jnp.dot(
        a_ref[...], w_ref[:, columns], preferred_element_type=jnp.float32
    ).astype(jnp.bfloat16)


def project_kernel(step, parts, a_ref, w_ref, *out_refs):
    for part, out_ref in zip(parts, out_refs):
        out_ref[...] = project_part(a_ref, w_ref, step, part)


def project(attended, weights, step, parts):
    width = sum(part.stop - part.start for part in parts)
    return pl.pallas_call(
        functools.partial(project_kernel, step, parts),
        out_shape=[part_shape(part) for part in parts],
        in_specs=[VMEM, VMEM],
        out_specs=[VMEM] * len(parts),
        compiler_params=pltpu.CompilerParams(vmem_limit_bytes=20 * MIB),
        cost_estimate=cost(2 * BLK * width * attended.shape[1], 1_000_000),
    )(attended, weights)


def part_shape(part):
    return jax.ShapeDtypeStruct((BLK, part.stop - part.start), jnp.bfloat16)


def close_kernel(parts, each, resume, *refs):
    refs = list(refs)
    mine_refs = [refs.pop(0) for _ in parts]
    other_refs = [[refs.pop(0) for _ in range(each)] for _ in parts]
    if resume:
        refs.pop(0)
    out_ref, *sum_refs, sems = refs
    copies = []
    for at, part in enumerate(parts):
        total = mine_refs[at][...].astype(jnp.float32)
        for ref in other_refs[at]:
            total = total + ref[...].astype(jnp.float32)
        sum_refs[at][...] = total.astype(sum_refs[at].dtype)
        copies.append(pltpu.make_async_copy(sum_refs[at], out_ref.at[:, part], sems.at[at]))
        copies[-1].start()
    for copy in copies:
        copy.wait()


def close(chosen, parts, mine, received, out=None):
    others = [row[at] for at in chosen for row in received]
    operands = [mine[at] for at in chosen] + others + ([] if out is None else [out])
    return pl.pallas_call(
        functools.partial(
            close_kernel, [parts[at] for at in chosen], len(received), out is not None
        ),
        out_shape=jax.ShapeDtypeStruct((BLK, parts[-1].stop), jnp.bfloat16),
        in_specs=[VMEM] * (len(chosen) + len(others)) + ([] if out is None else [HBM]),
        out_specs=HBM,
        scratch_shapes=[
            *[pltpu.VMEM((BLK, parts[at].stop - parts[at].start), jnp.bfloat16) for at in chosen],
            pltpu.SemaphoreType.DMA((len(chosen),)),
        ],
        input_output_aliases={} if out is None else {len(operands) - 1: 0},
        compiler_params=pltpu.CompilerParams(vmem_limit_bytes=8 * MIB),
        cost_estimate=cost(1_000_000, 1_000_000),
    )(*operands)


def mask_kernel(docs_ref, bias_ref):
    position = lax.axis_index("seq")
    doc = docs_ref[position]
    for at in range(bias_ref.shape[0]):
        near = (docs_ref[jnp.maximum(position - at - 1, 0)] == doc) & (position > at)
        bias_ref[at] = jnp.full(bias_ref.shape[1:], jnp.where(near, 0.0, FAR), jnp.float32)


def mask(docs, reach, rows):
    return pl.pallas_call(
        mask_kernel,
        out_shape=jax.ShapeDtypeStruct((reach, 1, rows), jnp.float32),
        in_specs=[SMEM],
        out_specs=VMEM,
    )(docs)


def side_by_side(left, right):
    low = jnp.array(-jnp.inf, left.dtype)
    first = lax.pad(left, low, ((0, 0, 0), (0, right.shape[1], 0)))
    return jnp.maximum(first, lax.pad(right, low, ((0, 0, 0), (left.shape[1], 0, 0))))


def local(query_states, key_states, value_states, out_weight, block_docs):
    tokens_here = query_states.shape[0]
    kv_local = key_states.shape[1] // HD
    group_size = QH // KH
    count = lax.axis_size("seq")
    groups = lax.axis_size("head")
    assert tokens_here == BLK and block_docs.shape[0] == count
    reach = min(DOC_BLK, count // 4) - 1
    eighth = out_weight.shape[1] // groups // 8
    ends = [eighth * sum(PARTS[:at]) for at in range(len(PARTS) + 1)]
    parts = [slice(begin, end) for begin, end in zip(ends, ends[1:])]
    sizes = (kv_local, group_size)

    kv = hold(side_by_side(key_states, value_states))
    if reach == 3 and count == len(RINGS[0]):
        packed, carrier = ring_table()
        first_kv = kv
        arrived = [lax.ppermute(kv, "seq", list(enumerate(ring))) for ring in RINGS[1:]]
        gaps = [functools.partial(pick, word) for word in packed]
        gaps.append(lambda position: 1 + 2 * (position & 1))
        state, bias, kv = opening(block_docs, query_states, kv, out_weight, gaps, *sizes)
        arrived = [lax.ppermute(first_kv, "seq", list(enumerate(RINGS[0])))] + arrived
        second = choose(carrier, arrived[1:], state[0])
        late = lax.ppermute(second, "seq", [(i, i ^ 1) for i in range(count)])
        state = attend(query_states, arrived[1:], bias, (1, 2), *sizes, state)
        attended, last = attend(
            query_states, [arrived[0], late], bias, (0, 3), *sizes, state, out_weight, parts[-1]
        )
    else:
        blocks = [kv]
        while len(blocks) < reach + 1:
            have = len(blocks)
            send = min(have, reach + 1 - have)
            passed = turned(jnp.stack(blocks[:send]), "seq", have)
            blocks = blocks + [passed[i] for i in range(send)]
        bias = mask(block_docs, reach, group_size * BLK)
        attended, last = attend(query_states, blocks, bias, tuple(range(reach)), *sizes, (), out_weight, parts[-1])

    received = []
    for step in range(1, groups):
        if step == 1:
            row = [*project(attended, out_weight, 1, parts[:-1]), last]
        else:
            row = project(attended, out_weight, step, parts)
        received.append([turned(partial, "head", step) for partial in row])
    mine = project(attended, out_weight, 0, parts)
    late = len(parts) - 2
    early = [at for at in range(len(parts)) if at != late]
    out = close(early, parts, mine, received)
    return close([late], parts, mine, received, out)


def solution(mesh):
    return jax.shard_map(
        local,
        mesh=mesh,
        in_specs=(P("seq", "head"), P("seq", "head"), P("seq", "head"), P("head", None), P()),
        out_specs=P("seq", "head"),
        check_vma=False,
    )
```
